32 devices in a mesh: groups: 2 (over x), lat: 16 (over z, y, core).
Axes of the slice: x: 2, y: 2, z: 4, core: 2. Of those that a mesh axis runs over, the one named last changes fastest.
Arguments:
- state_field: bfloat16 [96, 1440, 256], P(('groups', 'lat')), parts along dimension 0, may hold values from -6 to 6
- filter_values: float32 [48, 3, 2, 8, 3], P('lat'), may hold values from -0.8 to 0.8
- block_index: int32 [48, 3, 2], P('lat'), may hold values from 0 to 179
- disco_mix: bfloat16 [768, 256], replicated, may hold values from -0.21875 to 0.21875
- spectral_gain: float32 [48, 256], replicated, may hold values from 0.1 to 1.9
- spectral_weight: bfloat16 [2, 256, 256], replicated, may hold values from -0.25 to 0.25
Outputs:
- block_out: bfloat16 [96, 1440, 256], P(('groups', 'lat')), parts along dimension 0
The draws below stay inside these ranges and needn't reach their ends.
There are 2 independent parts, one for each index of `groups`. The reference program is written for one: setup_inputs(seed, part) draws one part's arguments, and reference() takes and returns one part's arrays. A program takes and returns all parts, laid end to end along the dimension named above; an argument that names none is the same for every part. Nothing has to cross between parts.
Inputs may be any that keep to these rules, and one draw needn't show every extreme that they name: `block_index`: block b stands for the longitude shifts 8 * b to 8 * b + 7; two entries of one cycle and offset may name the same block.
All inputs are finite; a program needn't handle non-finite values.
Results may differ from the reference program's by a relative error of at most 0.008.
Values may be sent and summed in bfloat16 or wider, within the bound.
A program may use at most 256 MiB of HBM per device.

```python
import math
import jax
import jax.numpy as jnp
from jax import lax

C = 256
NLON = 1440
KB = 3
NNZ = 2
SB = 8
NLAT = 48
LMAX = 48
MODES = 48


def plant(array, rng, low, top_value):
    longest = array.shape.index(max(array.shape))
    spots = []
    for shift in (0, 1):
        where = [jax.random.randint(jax.random.fold_in(rng, axis), (), 0, length) for axis, length in enumerate(array.shape)]
        where[longest] = (where[longest] + shift) % array.shape[longest]
        spots.append(tuple(where))
    return array.at[spots[0]].set(low).at[spots[1]].set(top_value)


def levels(stream_key, shape, pieces, smallest, top_value):
    level, own = 1.0, jax.random.fold_in(stream_key, 6)
    for axis_at, shards_of in pieces:
        draws = jnp.exp(jax.random.uniform(jax.random.fold_in(own, axis_at), (shards_of,), jnp.float32, smallest / len(pieces), top_value / len(pieces)))
        level = level * jnp.repeat(draws, shape[axis_at] // shards_of).reshape([-1 if axis == axis_at else 1 for axis in range(len(shape))])
    return level


def centred(stream_key, shape, scale, bound, pieces=(), kind=jnp.bfloat16):
    loudness = levels(stream_key, shape, pieces, -0.22, 0.18) if pieces else 1.0
    result = jax.random.normal(stream_key, shape, jnp.float32) * scale * loudness
    return jnp.minimum(jnp.maximum(result, -bound), bound).astype(kind)


def setup_inputs(seed: int = 0, part: int = 0) -> dict:
    splits = jax.random.split(jax.random.key(seed), 7)
    part_keys = jax.random.split(jax.random.fold_in(splits[6], part), 7)
    return {
        "state_field": centred(part_keys[0], (NLAT, NLON, C), 1.0, 6.0, ((0, 16),)),
        "filter_values": centred(splits[1], (NLAT, 3, NNZ, SB, KB), 0.144, 0.8, ((0, 16),), jnp.float32),
        "block_index": plant(jax.random.randint(splits[2], (NLAT, 3, NNZ), 0, NLON // SB), jax.random.fold_in(splits[2], 1), 0, (NLON // SB) - 1).astype(jnp.int32),
        "disco_mix": centred(splits[3], (KB * C, C), (KB * C) ** -0.5, 0.21875),
        "spectral_gain": jnp.clip(1.0 + 0.18 * jax.random.normal(splits[4], (LMAX, C), jnp.float32), 0.1, 1.9),
        "spectral_weight": centred(splits[5], (2, C, C), (2 * C) ** -0.5, 0.25),
    }


log_cut = -69.0

def legendre_table(wave_orders, degree_count, lat_count):
    colatitude = (jnp.arange(lat_count, dtype=jnp.float32) + 0.5) * (math.pi / lat_count)
    cosine = jnp.cos(colatitude)[None, :]
    sine_col = jnp.sin(colatitude)[None, :]
    orders = wave_orders.astype(jnp.float32)[:, None]
    log_first = 0.5 * (jnp.log(2.0 * orders + 1.0) - math.log(4.0 * math.pi)) + 0.5 * (lax.lgamma(orders + 0.5) - 0.5 * math.log(math.pi) - lax.lgamma(orders + 1.0)) + orders * jnp.log(sine_col)
    first_term = jnp.where(log_first < log_cut, 0.0, jnp.exp(log_first))

    def advance(state_pair, degree):
        before, current = state_pair
        deg_sq = degree * degree
        ord_sq = orders * orders
        lower_deg = degree - 1.0
        coef_up = jnp.sqrt((4.0 * deg_sq - 1.0) / jnp.maximum(deg_sq - ord_sq, 1.0))
        coef_down = jnp.sqrt(jnp.maximum(lower_deg * lower_deg - ord_sq, 0.0) / jnp.maximum(4.0 * lower_deg * lower_deg - 1.0, 1.0))
        general = coef_up * (cosine * current - coef_down * before)
        second = jnp.sqrt(2.0 * orders + 3.0) * cosine * current
        next_value = jnp.where(degree < orders, 0.0, jnp.where(degree == orders, first_term, jnp.where(degree == orders + 1.0, second, general)))
        return ((current, next_value), next_value)
    zeros_state = jnp.zeros((orders.shape[0], lat_count), jnp.float32)
    degrees = jnp.arange(degree_count, dtype=jnp.float32)
    final_state, table_rows = lax.scan(advance, (zeros_state, zeros_state), degrees)
    return jnp.transpose(table_rows, (1, 0, 2))

def quad_weights(lat_count):
    colatitude = (jnp.arange(lat_count, dtype=jnp.float32) + 0.5) * (math.pi / lat_count)
    return jnp.sin(colatitude) * (2.0 * math.pi * math.pi / lat_count)

def forward_table(waves, lon_count):
    longitude = jnp.arange(lon_count, dtype=jnp.int32)
    angles = (longitude[:, None] * waves[None, :] % lon_count).astype(jnp.float32) * (2.0 * math.pi / lon_count)
    paired = jnp.stack([jnp.cos(angles), -jnp.sin(angles)], axis=2) / lon_count
    return paired.reshape(lon_count, 2 * waves.shape[0]).astype(jnp.bfloat16)

def inverse_table(waves, lon_count):
    longitude = jnp.arange(lon_count, dtype=jnp.int32)
    angles = (waves[:, None] * longitude[None, :] % lon_count).astype(jnp.float32) * (2.0 * math.pi / lon_count)
    factor = jnp.where(waves == 0, 1.0, 2.0).astype(jnp.float32)[:, None]
    paired = jnp.stack([factor * jnp.cos(angles), -factor * jnp.sin(angles)], axis=1)
    return paired.reshape(2 * waves.shape[0], lon_count).astype(jnp.bfloat16)

def offset_terms(sources, filters, blocks, lon_count, shift_block):
    summed = None

    def cut_window(cycle_data, first_cell):
        return lax.dynamic_slice_in_dim(cycle_data, first_cell, lon_count + shift_block - 1, 0)
    for block_slot in range(blocks.shape[1]):
        starts = (lon_count - blocks[:, block_slot] * shift_block - (shift_block - 1)).astype(jnp.int32)
        window = jax.vmap(cut_window)(sources, starts)
        for shift in range(shift_block):
            shifted = window[:, shift_block - 1 - shift:shift_block - 1 - shift + lon_count, None, :]
            weight_now = filters[:, block_slot, shift, :][:, None, :, None]
            product_term = weight_now * shifted
            summed = product_term if summed is None else summed + product_term
    return summed

def reference(state_field, filter_values, block_index, disco_mix, spectral_gain, spectral_weight):
    padded = jnp.pad(state_field, ((1, 1), (0, 0), (0, 0)))
    doubled = jnp.concatenate([padded, padded], axis=1)
    group_rows = 8

    def mix_group(group_index):
        first_row = (group_index * group_rows).astype(jnp.int32)
        sources = lax.dynamic_slice_in_dim(doubled, first_row, group_rows + 2, 0)
        filters = lax.dynamic_slice_in_dim(filter_values, first_row, group_rows, 0)
        blocks = lax.dynamic_slice_in_dim(block_index, first_row, group_rows, 0)
        summed = offset_terms(sources[0:group_rows], filters[:, 0], blocks[:, 0], NLON, SB)
        summed = summed + offset_terms(sources[1:group_rows + 1], filters[:, 1], blocks[:, 1], NLON, SB)
        summed = summed + offset_terms(sources[2:group_rows + 2], filters[:, 2], blocks[:, 2], NLON, SB)
        basis_terms = summed.reshape(group_rows, NLON, KB * C).astype(jnp.bfloat16)
        return jnp.einsum('rlk,kc->rlc', basis_terms.astype(jnp.float32), disco_mix.astype(jnp.float32)).astype(jnp.bfloat16)
    local_mix = lax.map(mix_group, jnp.arange(NLAT // group_rows, dtype=jnp.int32)).reshape(NLAT, NLON, C)
    waves = jnp.arange(MODES, dtype=jnp.int32)
    table_fwd = forward_table(waves, NLON)
    spectrum = jnp.einsum('lq,rlc->rqc', table_fwd.astype(jnp.float32), local_mix.astype(jnp.float32)).astype(jnp.bfloat16)
    legendre = legendre_table(waves, LMAX, NLAT)
    quadrature = quad_weights(NLAT)
    per_mode_data = jnp.transpose(spectrum.reshape(NLAT, MODES, 2 * C), (1, 0, 2))

    def per_mode(operands):
        slot_table, slot_data = operands
        weighted = slot_table * quadrature[None, :]
        coefficients = jnp.dot(weighted, slot_data.astype(jnp.float32), precision=lax.Precision.HIGHEST)
        scaled = (coefficients.reshape(LMAX, 2, C) * spectral_gain[:, None, :]).astype(jnp.bfloat16)
        real_in = scaled[:, 0, :]
        imag_in = scaled[:, 1, :]
        mixed_real = jnp.dot(real_in, spectral_weight[0], preferred_element_type=jnp.float32) - jnp.dot(imag_in, spectral_weight[1], preferred_element_type=jnp.float32)
        mixed_imag = jnp.dot(real_in, spectral_weight[1], preferred_element_type=jnp.float32) + jnp.dot(imag_in, spectral_weight[0], preferred_element_type=jnp.float32)
        mixed_rows = jnp.concatenate([mixed_real, mixed_imag], axis=1)
        return jnp.dot(slot_table.T, mixed_rows, precision=lax.Precision.HIGHEST).astype(jnp.bfloat16)
    synthesis = lax.map(per_mode, (legendre, per_mode_data))
    synthesis = jnp.transpose(synthesis, (1, 0, 2)).reshape(NLAT, 2 * MODES, C)
    table_inv = inverse_table(waves, NLON)
    global_part = jnp.einsum('rqc,ql->rlc', synthesis.astype(jnp.float32), table_inv.astype(jnp.float32))
    return jax.nn.gelu(local_mix.astype(jnp.float32) + global_part).astype(jnp.bfloat16)
```

```python
import functools
import math

import jax
import jax.numpy as jnp
import ml_dtypes
import numpy as np
from jax import lax
from jax.experimental import pallas as pl
from jax.experimental.pallas import tpu as pltpu
from jax.sharding import PartitionSpec as P

M_DEV = 3
KB = 3
SB = 8
ROWS = 96
WIN = 128
CHUNK = 48
BLK = 32
log_cut = -69.0
MESH = pl.DeviceIdType.MESH
F32 = jnp.float32
BF16 = jnp.bfloat16


def legendre_np(count):
    theta = (np.arange(count) + 0.5) * (math.pi / count)
    cosine, sine = np.cos(theta)[None], np.sin(theta)[None]
    m = np.arange(count, dtype=np.float64)[:, None]
    lg = np.array([math.lgamma(x + 0.5) - math.lgamma(x + 1.0) for x in range(count)])[:, None]
    g = 0.5 * (np.log(2 * m + 1) - math.log(4 * math.pi)) + 0.5 * (lg - 0.5 * math.log(math.pi)) + m * np.log(sine)
    first = np.where(g < log_cut, 0.0, np.exp(g))
    table = np.zeros((count, count, count))
    before = current = np.zeros((count, count))
    for l in range(count):
        up = np.sqrt((4.0 * l * l - 1.0) / np.maximum(l * l - m * m, 1.0)) if l else 0.0 * m
        down = np.sqrt(np.maximum((l - 1.0) ** 2 - m * m, 0.0) / max(4.0 * (l - 1.0) ** 2 - 1.0, 1.0))
        general = up * (cosine * current - down * before)
        second = np.sqrt(2 * m + 3) * cosine * current
        value = np.where(l < m, 0.0, np.where(l == m, first, np.where(l == m + 1, second, general)))
        before, current = current, value
        table[:, l] = value
    return table


def legendre_table(wave_orders, degree_count, lat_count):
    colatitude = (jnp.arange(lat_count, dtype=F32) + 0.5) * (math.pi / lat_count)
    cosine = jnp.cos(colatitude)[None, :]
    sine_col = jnp.sin(colatitude)[None, :]
    orders = wave_orders.astype(F32)[:, None]
    log_first = (
        0.5 * (jnp.log(2.0 * orders + 1.0) - math.log(4.0 * math.pi))
        + 0.5 * (lax.lgamma(orders + 0.5) - 0.5 * math.log(math.pi) - lax.lgamma(orders + 1.0))
        + orders * jnp.log(sine_col)
    )
    first_term = jnp.where(log_first < log_cut, 0.0, jnp.exp(log_first))

    def advance(state_pair, degree):
        before, current = state_pair
        deg_sq = degree * degree
        ord_sq = orders * orders
        lower_deg = degree - 1.0
        coef_up = jnp.sqrt(jnp.maximum(4.0 * deg_sq - 1.0, 0.0) / jnp.maximum(deg_sq - ord_sq, 1.0))
        coef_down = jnp.sqrt(
            jnp.maximum(lower_deg * lower_deg - ord_sq, 0.0)
            / jnp.maximum(4.0 * lower_deg * lower_deg - 1.0, 1.0)
        )
        general = coef_up * (cosine * current - coef_down * before)
        second = jnp.sqrt(2.0 * orders + 3.0) * cosine * current
        next_value = jnp.where(
            degree < orders,
            0.0,
            jnp.where(
                degree == orders, first_term, jnp.where(degree == orders + 1.0, second, general)
            ),
        )
        return ((current, next_value), next_value)

    zeros_state = jnp.zeros((orders.shape[0], lat_count), F32)
    degrees = jnp.arange(degree_count, dtype=F32)
    _, table_rows = lax.scan(advance, (zeros_state, zeros_state), degrees)
    return jnp.transpose(table_rows, (1, 0, 2))


def spread(xp, table, quad, devices):
    count = table.shape[1]
    chunks = count // CHUNK
    lat = xp.arange(count)[:, None]
    col = xp.arange(devices * BLK)[None, :]
    here = (lat == 3 * (col // BLK) + col % BLK // 8) & (col % BLK < 24)

    def lay(values):
        if xp is jnp:
            values = values.astype(BF16)
        rows = []
        for p in range(2):
            for m in range(M_DEV):
                pick = (here & (col % 8 == 2 * m + p)).astype(values.dtype)
                rows.append(xp.matmul(values[m], pick).reshape(chunks, 1, CHUNK, devices * BLK))
        return xp.concatenate(rows, axis=1).reshape(chunks, 2 * M_DEV * CHUNK, devices * BLK)

    return lay(table * quad[None, None, :]), lay(table).transpose(0, 2, 1)


def constants(devices, lon):
    modes = M_DEV * devices
    angle = (np.arange(modes)[:, None] * np.arange(lon)[None, :] % lon) * (2.0 * math.pi / lon)
    factor = np.where(np.arange(modes) == 0, 1.0, 2.0)[:, None]

    def pad(re, im):
        paired = np.stack([re, im], axis=1).reshape(devices, 2 * M_DEV, lon)
        return np.pad(paired, ((0, 0), (0, 2), (0, 0))).reshape(devices * 8, lon)

    bf = ml_dtypes.bfloat16
    fwd = pad(np.cos(angle) / lon, -np.sin(angle) / lon).astype(np.float32).astype(bf)
    inv = pad(factor * np.cos(angle), -factor * np.sin(angle)).T.astype(np.float32).astype(bf)
    return fwd, inv


def toeplitz(f_ref, b_ref, cycle, offset, slot):
    which = (cycle * 3 + offset) * 2 + slot
    odd = lax.rem(b_ref[which], 2)
    shape = (ROWS, WIN)
    delta = (
        lax.broadcasted_iota(jnp.int32, shape, 0)
        - lax.broadcasted_iota(jnp.int32, shape, 1)
        + (16 - 8 * odd)
    )
    parts = [jnp.zeros(shape, F32) for _ in range(KB)]
    for t in range(SB):
        hit = delta == t
        for k in range(KB):
            parts[k] = jnp.where(hit, f_ref[(which * SB + t) * KB + k], parts[k])
    return [part.astype(BF16) for part in parts]


def window_start(b_ref, cycle, offset, slot, first, lon):
    half = b_ref[(cycle * 3 + offset) * 2 + slot] // 2
    start = first + lon - 16 - 16 * half
    start = jnp.where(start >= lon, start - lon, start)
    return pl.multiple_of(start, 16)


def mix_tile(basis, mix_ref):
    basis = basis.astype(BF16)
    wide = jnp.concatenate([basis[k * ROWS : (k + 1) * ROWS] for k in range(KB)], axis=1)
    return jnp.dot(wide, mix_ref[...], preferred_element_type=F32)


def fill_toeplitz(t_ref, f_ref, b_ref, cycle, offset, column):
    for slot in range(2):
        parts = toeplitz(f_ref, b_ref, cycle, offset, slot)
        for k in range(KB):
            t_ref[k * ROWS : (k + 1) * ROWS, (column + slot) * WIN : (column + slot + 1) * WIN] = parts[k]


def inner_kernel(f_ref, b_ref, x_ref, mix_ref, fwd_ref, loc_ref, part_ref, th_ref, spec_ref, ext, t0, t1, t2):
    lon = x_ref.shape[1]
    for i in range(3):
        ext[i, 0:lon] = x_ref[i]
        ext[i, lon : lon + WIN] = x_ref[i, 0:WIN]
    plan = {0: ((0, 1), (1, 2)), 1: ((0, 0), (1, 1), (2, 2)), 2: ((1, 0), (2, 1))}
    tables = (t0, t1, t2)
    for i in range(3):
        for n, (_, offset) in enumerate(plan[i]):
            fill_toeplitz(tables[i], f_ref, b_ref, i, offset, 2 * n)
    fill_toeplitz(th_ref.at[0], f_ref, b_ref, 0, 0, 0)
    fill_toeplitz(th_ref.at[1], f_ref, b_ref, 2, 2, 0)

    def tile(a, carry):
        first = pl.multiple_of(a * ROWS, 16)
        for i in range(3):
            pieces = []
            for source, offset in plan[i]:
                for slot in range(2):
                    start = window_start(b_ref, i, offset, slot, first, lon)
                    pieces.append(ext[source, pl.ds(start, WIN), :])
            basis = jnp.dot(tables[i][...], jnp.concatenate(pieces, axis=0), preferred_element_type=F32)
            out = mix_tile(basis, mix_ref)
            if i == 1:
                loc_ref[pl.ds(first, ROWS), :] = out.astype(BF16)
            else:
                part_ref[i // 2, pl.ds(first, ROWS), :] = out
        return carry

    lax.fori_loop(0, lon // ROWS, tile, 0)
    spec_ref[...] = jnp.dot(fwd_ref[...], loc_ref[...], preferred_element_type=F32)


def outer_kernel(b_ref, north_ref, south_ref, th_ref, part_ref, spec_ref, mix_ref, fwd_ref, loc_ref, x_ref, ext):
    lon = north_ref.shape[0]
    for h, ref in enumerate((north_ref, south_ref)):
        ext[h, 0:lon] = ref[...]
        ext[h, lon : lon + WIN] = ref[0:WIN]

    def tile(a, carry):
        first = pl.multiple_of(a * ROWS, 16)
        for h in range(2):
            pieces = []
            for slot in range(2):
                start = window_start(b_ref, 2 * h, 2 * h, slot, first, lon)
                pieces.append(ext[h, pl.ds(start, WIN), :])
            basis = jnp.dot(th_ref[h], jnp.concatenate(pieces, axis=0), preferred_element_type=F32)
            out = mix_tile(basis, mix_ref) + part_ref[h, pl.ds(first, ROWS), :]
            loc_ref[h, pl.ds(first, ROWS), :] = out.astype(BF16)
        return carry

    lax.fori_loop(0, lon // ROWS, tile, 0)
    s0 = jnp.dot(fwd_ref[...], loc_ref[0], preferred_element_type=F32)
    s2 = jnp.dot(fwd_ref[...], loc_ref[1], preferred_element_type=F32)
    devices = x_ref.shape[0]
    three = [s.reshape(devices, 8, s.shape[1]) for s in (s0, spec_ref[...], s2)]
    three.append(jnp.zeros_like(three[0]))
    x_ref[...] = jnp.concatenate(three, axis=1).astype(BF16)


def spectral_kernel(
    devices, x_ref, ana_hbm, syn_hbm, gain_ref, w_ref, out_ref,
    recv, back, ret, ana, syn, wide, acc, load_sem, send_a, recv_a, send_b, recv_b,
):
    me = lax.axis_index("lat")
    chunks = ana_hbm.shape[1]
    mine = me if ana_hbm.shape[0] > 1 else 0
    width = w_ref.shape[1]
    half = M_DEV * CHUNK

    def load(ch):
        return (
            pltpu.make_async_copy(ana_hbm.at[mine, ch], ana, load_sem.at[0]),
            pltpu.make_async_copy(syn_hbm.at[mine, ch], syn, load_sem.at[1]),
        )

    for c in load(0):
        c.start()
    barrier = pltpu.get_barrier_semaphore()

    def greet(s, carry):
        pl.semaphore_signal(barrier, inc=1, device_id={"lat": lax.rem(me + s, devices)}, device_id_type=MESH)
        return carry

    lax.fori_loop(1, devices, greet, 0)
    pl.semaphore_wait(barrier, devices - 1)

    def remote(src, dst, ssem, rsem, s, to, row):
        return pltpu.make_async_remote_copy(
            src_ref=src.at[to], dst_ref=dst.at[row], send_sem=ssem.at[s], recv_sem=rsem.at[row],
            device_id={"lat": to}, device_id_type=MESH,
        )

    def start_all(src, dst, ssem, rsem):
        def one(s, carry):
            remote(src, dst, ssem, rsem, s, lax.rem(me + s, devices), me).start()
            return carry

        lax.fori_loop(1, devices, one, 0)
        dst[me] = src[me]

    def wait_all(src, dst, ssem, rsem, send):
        def one(s, carry):
            peer = lax.rem(me + s, devices)
            copy = remote(src, dst, ssem, rsem, s, peer, peer)
            if send:
                copy.wait_send()
            else:
                copy.wait_recv()
            return carry

        lax.fori_loop(1, devices, one, 0)

    start_all(x_ref, recv, send_a, recv_a)
    wide[0:width, 0:width] = w_ref[0]
    wide[0:width, width:] = w_ref[1]
    wide[width:, 0:width] = -w_ref[1]
    wide[width:, width:] = w_ref[0]
    acc[...] = jnp.zeros_like(acc)
    wait_all(x_ref, recv, send_a, recv_a, False)

    rows = 16 * BLK

    def chunk(ch, carry):
        for c in load(ch):
            c.wait()
        data = recv[...].reshape(devices * BLK, width)
        coef = jnp.dot(ana[...], data, preferred_element_type=F32)
        gain = gain_ref[pl.ds(pl.multiple_of(ch * CHUNK, CHUNK), CHUNK), :]
        gain = jnp.concatenate([gain] * M_DEV, axis=0)
        scaled = jnp.concatenate([coef[:half] * gain, coef[half:] * gain], axis=1).astype(BF16)
        mixed = jnp.dot(scaled, wide[...], preferred_element_type=F32).astype(BF16)
        stacked = jnp.concatenate([mixed[:, :width], mixed[:, width:]], axis=0)

        def piece(r, inner):
            at = pl.ds(pl.multiple_of(r * rows, rows), rows)
            acc[at, :] += jnp.dot(syn[at, :], stacked, preferred_element_type=F32)
            return inner

        lax.fori_loop(0, devices * BLK // rows, piece, 0)

        @pl.when(ch + 1 < chunks)
        def _():
            for c in load(ch + 1):
                c.start()

        return carry

    lax.fori_loop(0, chunks, chunk, 0)
    back[...] = acc[...].reshape(devices, BLK, width).astype(BF16)
    start_all(back, ret, send_b, recv_b)
    wait_all(x_ref, recv, send_a, recv_a, True)
    wait_all(back, ret, send_b, recv_b, False)
    got = ret[...].astype(F32)
    for i in range(3):
        out_ref[i] = got[:, 8 * i : 8 * i + 8, :].reshape(devices * 8, width).astype(BF16)
    wait_all(back, ret, send_b, recv_b, True)


def final_kernel(mid_ref, edge_ref, modes_ref, inv_ref, out_ref):
    part = jnp.dot(inv_ref[...], modes_ref[0], preferred_element_type=F32)
    local = jnp.where(pl.program_id(0) == 1, mid_ref[...], edge_ref[0])
    out_ref[0] = jax.nn.gelu(local.astype(F32) + part).astype(BF16)


def body(devices, fwd_np, inv_np, leg_np, state, filters, blocks, mix, gain, weight):
    cycles, lon, ch = state.shape
    lat_count = cycles * devices
    chunks = lat_count // CHUNK
    fwd, inv = jnp.asarray(fwd_np), jnp.asarray(inv_np)
    up = [(i, i + 1) for i in range(devices - 1)]
    down = [(i + 1, i) for i in range(devices - 1)]
    north = lax.ppermute(state[cycles - 1], "lat", up)
    south = lax.ppermute(state[0], "lat", down)
    if leg_np is not None:
        ana, syn = jnp.asarray(leg_np[0]), jnp.asarray(leg_np[1])
    else:
        own = lax.axis_index("lat") * M_DEV + jnp.arange(M_DEV, dtype=jnp.int32)
        theta = (jnp.arange(lat_count, dtype=F32) + 0.5) * (math.pi / lat_count)
        quad = jnp.sin(theta) * (2.0 * math.pi * math.pi / lat_count)
        ana, syn = spread(jnp, legendre_table(own, lat_count, lat_count), quad, devices)
        ana, syn = ana.astype(BF16)[None], syn.astype(BF16)[None]

    vmem = pl.BlockSpec(memory_space=pltpu.VMEM)
    smem = pl.BlockSpec(memory_space=pltpu.SMEM)
    hbm = pl.BlockSpec(memory_space=pl.ANY)
    shape = jax.ShapeDtypeStruct
    fl, bl = filters.reshape(-1), blocks.reshape(-1)
    params = functools.partial(pltpu.CompilerParams, vmem_limit_bytes=48 * 2**20)
    loc1, part, th, spec1 = pl.pallas_call(
        inner_kernel,
        out_shape=(
            shape((lon, ch), BF16),
            shape((2, lon, ch), F32),
            shape((2, KB * ROWS, 2 * WIN), BF16),
            shape((devices * 8, ch), F32),
        ),
        in_specs=[smem, smem, vmem, vmem, vmem],
        out_specs=(vmem,) * 4,
        scratch_shapes=[
            pltpu.VMEM((3, lon + WIN, ch), BF16),
            pltpu.VMEM((KB * ROWS, 4 * WIN), BF16),
            pltpu.VMEM((KB * ROWS, 6 * WIN), BF16),
            pltpu.VMEM((KB * ROWS, 4 * WIN), BF16),
        ],
        compiler_params=params(),
        cost_estimate=pl.CostEstimate(flops=10**10, bytes_accessed=10**7, transcendentals=0),
        name="inner",
    )(fl, bl, state, mix, fwd)
    edges, xbuf = pl.pallas_call(
        outer_kernel,
        out_shape=(shape((2, lon, ch), BF16), shape((devices, BLK, ch), BF16)),
        in_specs=[smem] + [vmem] * 7,
        out_specs=(vmem, vmem),
        scratch_shapes=[pltpu.VMEM((2, lon + WIN, ch), BF16)],
        compiler_params=params(),
        name="outer",
    )(bl, north, south, th, part, spec1, mix, fwd)
    block = pltpu.VMEM((devices, BLK, ch), BF16)
    rows = 2 * M_DEV * CHUNK
    sems = pltpu.SemaphoreType.DMA((devices,))
    modes = pl.pallas_call(
        functools.partial(spectral_kernel, devices),
        out_shape=shape((3, devices * 8, ch), BF16),
        in_specs=[vmem, hbm, hbm, vmem, vmem],
        out_specs=vmem,
        scratch_shapes=[
            block, block, block,
            pltpu.VMEM((rows, devices * BLK), BF16),
            pltpu.VMEM((devices * BLK, rows), BF16),
            pltpu.VMEM((2 * ch, 2 * ch), BF16),
            pltpu.VMEM((devices * BLK, ch), F32),
            pltpu.SemaphoreType.DMA((2,)),
            sems, sems, sems, sems,
        ],
        compiler_params=params(collective_id=0, has_side_effects=True),
        name="spectral",
    )(xbuf, ana, syn, gain, weight)
    step = 480
    return pl.pallas_call(
        final_kernel,
        grid=(3, lon // step),
        out_shape=shape((cycles, lon, ch), BF16),
        in_specs=[
            pl.BlockSpec((step, ch), lambda i, n: (jnp.where(i == 1, n, jnp.where(i == 0, 0, lon // step - 1)), 0)),
            pl.BlockSpec((1, step, ch), lambda i, n: (i // 2, jnp.where(i == 1, lon // step - 1, n), 0)),
            pl.BlockSpec((1, devices * 8, ch), lambda i, n: (i, 0, 0)),
            pl.BlockSpec((step, devices * 8), lambda i, n: (n, 0)),
        ],
        out_specs=pl.BlockSpec((1, step, ch), lambda i, n: (i, n, 0)),
        compiler_params=params(),
        name="final",
    )(loc1, edges, modes, inv)


def solution(mesh):
    devices = mesh.shape["lat"]
    lon = 1440
    fwd, inv = constants(devices, lon)
    count = M_DEV * devices
    leg = None
    if count <= 96:
        table = legendre_np(count)
        quad = np.sin((np.arange(count) + 0.5) * (math.pi / count)) * (2.0 * math.pi**2 / count)
        pairs = [spread(np, table[M_DEV * d : M_DEV * d + M_DEV], quad, devices) for d in range(devices)]
        leg = [np.stack([p[n] for p in pairs]).astype(np.float32).astype(ml_dtypes.bfloat16) for n in range(2)]
    return jax.shard_map(
        functools.partial(body, devices, fwd, inv, leg),
        mesh=mesh,
        in_specs=(
            P(("groups", "lat"), None, None),
            P("lat", None, None, None, None),
            P("lat", None, None),
            P(),
            P(),
            P(),
        ),
        out_specs=P(("groups", "lat"), None, None),
        check_vma=False,
    )
```

```python
import functools
import math

import jax
import jax.numpy as jnp
import ml_dtypes
import numpy as np
from jax import lax
from jax.experimental import pallas as pl
from jax.experimental.pallas import tpu as pltpu
from jax.sharding import PartitionSpec as P

M_DEV = 3
KB = 3
SB = 8
ROWS = 48
WIN = 64
CHUNK = 48
BLK = 32
log_cut = -69.0
MESH = pl.DeviceIdType.MESH
F32 = jnp.float32
BF16 = jnp.bfloat16


def legendre_np(count):
    theta = (np.arange(count) + 0.5) * (math.pi / count)
    cosine, sine = np.cos(theta)[None], np.sin(theta)[None]
    m = np.arange(count, dtype=np.float64)[:, None]
    lg = np.array([math.lgamma(x + 0.5) - math.lgamma(x + 1.0) for x in range(count)])[:, None]
    g = 0.5 * (np.log(2 * m + 1) - math.log(4 * math.pi)) + 0.5 * (lg - 0.5 * math.log(math.pi)) + m * np.log(sine)
    first = np.where(g < log_cut, 0.0, np.exp(g))
    table = np.zeros((count, count, count))
    before = current = np.zeros((count, count))
    for l in range(count):
        up = np.sqrt((4.0 * l * l - 1.0) / np.maximum(l * l - m * m, 1.0)) if l else 0.0 * m
        down = np.sqrt(np.maximum((l - 1.0) ** 2 - m * m, 0.0) / max(4.0 * (l - 1.0) ** 2 - 1.0, 1.0))
        general = up * (cosine * current - down * before)
        second = np.sqrt(2 * m + 3) * cosine * current
        value = np.where(l < m, 0.0, np.where(l == m, first, np.where(l == m + 1, second, general)))
        before, current = current, value
        table[:, l] = value
    return table


def legendre_table(wave_orders, degree_count, lat_count):
    colatitude = (jnp.arange(lat_count, dtype=F32) + 0.5) * (math.pi / lat_count)
    cosine = jnp.cos(colatitude)[None, :]
    sine_col = jnp.sin(colatitude)[None, :]
    orders = wave_orders.astype(F32)[:, None]
    log_first = (
        0.5 * (jnp.log(2.0 * orders + 1.0) - math.log(4.0 * math.pi))
        + 0.5 * (lax.lgamma(orders + 0.5) - 0.5 * math.log(math.pi) - lax.lgamma(orders + 1.0))
        + orders * jnp.log(sine_col)
    )
    first_term = jnp.where(log_first < log_cut, 0.0, jnp.exp(log_first))

    def advance(state_pair, degree):
        before, current = state_pair
        deg_sq = degree * degree
        ord_sq = orders * orders
        lower_deg = degree - 1.0
        coef_up = jnp.sqrt(jnp.maximum(4.0 * deg_sq - 1.0, 0.0) / jnp.maximum(deg_sq - ord_sq, 1.0))
        coef_down = jnp.sqrt(
            jnp.maximum(lower_deg * lower_deg - ord_sq, 0.0)
            / jnp.maximum(4.0 * lower_deg * lower_deg - 1.0, 1.0)
        )
        general = coef_up * (cosine * current - coef_down * before)
        second = jnp.sqrt(2.0 * orders + 3.0) * cosine * current
        next_value = jnp.where(
            degree < orders,
            0.0,
            jnp.where(
                degree == orders, first_term, jnp.where(degree == orders + 1.0, second, general)
            ),
        )
        return ((current, next_value), next_value)

    zeros_state = jnp.zeros((orders.shape[0], lat_count), F32)
    degrees = jnp.arange(degree_count, dtype=F32)
    _, table_rows = lax.scan(advance, (zeros_state, zeros_state), degrees)
    return jnp.transpose(table_rows, (1, 0, 2))


def spread(xp, table, quad, devices):
    count = table.shape[1]
    chunks = count // CHUNK
    lat = xp.arange(count)[:, None]
    col = xp.arange(devices * BLK)[None, :]
    here = (lat == 3 * (col // BLK) + col % BLK // 8) & (col % BLK < 24)

    def lay(values):
        if xp is jnp:
            values = values.astype(BF16)
        rows = []
        for p in range(2):
            for m in range(M_DEV):
                pick = (here & (col % 8 == 2 * m + p)).astype(values.dtype)
                rows.append(xp.matmul(values[m], pick).reshape(chunks, 1, CHUNK, devices * BLK))
        return xp.concatenate(rows, axis=1).reshape(chunks, 2 * M_DEV * CHUNK, devices * BLK)

    return lay(table * quad[None, None, :]), lay(table).transpose(0, 2, 1)


def constants(devices, lon):
    modes = M_DEV * devices
    angle = (np.arange(modes)[:, None] * np.arange(lon)[None, :] % lon) * (2.0 * math.pi / lon)
    factor = np.where(np.arange(modes) == 0, 1.0, 2.0)[:, None]

    def pad(re, im):
        paired = np.stack([re, im], axis=1).reshape(devices, 2 * M_DEV, lon)
        return np.pad(paired, ((0, 0), (0, 2), (0, 0))).reshape(devices * 8, lon)

    bf = ml_dtypes.bfloat16
    fwd = pad(np.cos(angle) / lon, -np.sin(angle) / lon).astype(np.float32).astype(bf)
    inv = pad(factor * np.cos(angle), -factor * np.sin(angle)).T.astype(np.float32).astype(bf)
    return fwd, inv


def fill_toeplitz(t_ref, f_ref, o_ref, cycle, offset, column):
    shape = (ROWS, 2 * WIN)
    lane = lax.broadcasted_iota(jnp.int32, shape, 1)
    first_slot = lane < WIN
    off = [o_ref[cycle, slot, offset] for slot in range(2)]
    delta = (
        lax.broadcasted_iota(jnp.int32, shape, 0)
        + jnp.where(first_slot, off[0], off[1] + WIN)
        - lane
    )
    parts = [jnp.zeros(shape, F32) for _ in range(KB)]
    for t in range(SB):
        hit = delta == t
        for k in range(KB):
            value = jnp.where(first_slot, f_ref[cycle, offset, k, 0, t], f_ref[cycle, offset, k, 1, t])
            parts[k] = jnp.where(hit, value, parts[k])
    for k in range(KB):
        t_ref[cycle, k * ROWS : (k + 1) * ROWS, column * 2 * WIN : (column + 1) * 2 * WIN] = parts[k].astype(BF16)


def windows(b_ref, ref, cycle, offset, a):
    pieces = []
    for slot in range(2):
        row = b_ref[cycle, slot, offset] + a * (ROWS // 16)
        pieces += [ref[row + n] for n in range(WIN // 16)]
    return pieces


def main_kernel(
    devices, f_ref, b_ref, o_ref, x_hbm, mix_ref, fwd_ref, ana_hbm, syn_hbm, gain_ref, w_ref,
    loc_ref, out_ref,
    e0, e1, e2, north, south, tab, bas, part, spec1,
    x_ref, recv, back, ret, ana, syn, wide, acc,
    load_sem, x_sem, halo_send, halo_recv, send_a, recv_a, send_b, recv_b,
):
    me = lax.axis_index("lat")
    tiles = x_hbm.shape[1]
    lon = tiles * 16
    chunks = ana_hbm.shape[1]
    mine = me if ana_hbm.shape[0] > 1 else 0
    width = w_ref.shape[1]
    half = M_DEV * CHUNK

    barrier = pltpu.get_barrier_semaphore()

    def greet(s, carry):
        pl.semaphore_signal(barrier, inc=1, device_id={"lat": lax.rem(me + s, devices)}, device_id_type=MESH)
        return carry

    lax.fori_loop(1, devices, greet, 0)

    held = (e0, e1, e2)
    fetches = []
    for i in range(3):
        fetches.append(pltpu.make_async_copy(x_hbm.at[i], held[i].at[pl.ds(0, tiles)], x_sem.at[2 * i]))
        fetches.append(
            pltpu.make_async_copy(x_hbm.at[i], held[i].at[pl.ds(tiles, tiles)], x_sem.at[2 * i + 1])
        )
    for c in fetches:
        c.start()

    def load(ch):
        return (
            pltpu.make_async_copy(ana_hbm.at[mine, ch], ana, load_sem.at[0]),
            pltpu.make_async_copy(syn_hbm.at[mine, ch], syn, load_sem.at[1]),
        )

    for c in load(0):
        c.start()
    pl.semaphore_wait(barrier, devices - 1)

    send_up = pltpu.make_async_remote_copy(
        src_ref=x_hbm.at[2], dst_ref=north.at[pl.ds(0, tiles)], send_sem=halo_send.at[0], recv_sem=halo_recv.at[0],
        device_id={"lat": lax.rem(me + 1, devices)}, device_id_type=MESH,
    )
    send_down = pltpu.make_async_remote_copy(
        src_ref=x_hbm.at[0], dst_ref=south.at[pl.ds(0, tiles)], send_sem=halo_send.at[1], recv_sem=halo_recv.at[1],
        device_id={"lat": lax.rem(me + devices - 1, devices)}, device_id_type=MESH,
    )

    @pl.when(me < devices - 1)
    def _():
        send_up.start()

    @pl.when(me > 0)
    def _():
        send_down.start()

    plan = {0: ((0, 1), (1, 2)), 1: ((0, 0), (1, 1), (2, 2)), 2: ((1, 0), (2, 1))}
    for i in range(3):
        for n, (_, offset) in enumerate(plan[i]):
            fill_toeplitz(tab, f_ref, o_ref, i, offset, n)
    fill_toeplitz(tab, f_ref, o_ref, 0, 0, 2)
    fill_toeplitz(tab, f_ref, o_ref, 2, 2, 2)
    wide[0:width, 0:width] = w_ref[0]
    wide[0:width, width:] = w_ref[1]
    wide[width:, 0:width] = -w_ref[1]
    wide[width:, width:] = w_ref[0]
    acc[...] = jnp.zeros_like(acc)
    for c in fetches:
        c.wait()

    def keep(i, first, basis):
        basis = basis.astype(BF16)
        for k in range(KB):
            bas[i, pl.ds(first, ROWS), k * width : (k + 1) * width] = basis[k * ROWS : (k + 1) * ROWS]

    def inner(a, carry):
        first = pl.multiple_of(a * ROWS, 16)
        for i in range(3):
            pieces = []
            for source, offset in plan[i]:
                pieces += windows(b_ref, held[source], i, offset, a)
            used = len(pieces) * 16
            basis = jnp.dot(tab[i, :, 0:used], jnp.concatenate(pieces, axis=0), preferred_element_type=F32)
            if i == 1:
                keep(i, first, basis)
            else:
                part[i // 2, a] = basis
        return carry

    lax.fori_loop(0, lon // ROWS, inner, 0)

    step = lon // 3

    def mix_cycle(i):
        def one(n, carry):
            at = pl.ds(pl.multiple_of(n * step, 16), step)
            loc_ref[i, at, :] = jnp.dot(bas[i, at, :], mix_ref[...], preferred_element_type=F32).astype(BF16)
            return carry

        lax.fori_loop(0, 3, one, 0)
        return jnp.dot(fwd_ref[...], loc_ref[i], preferred_element_type=F32)

    spec1[...] = mix_cycle(1)

    for ref, inside, copy in ((north, me > 0, send_up), (south, me < devices - 1, send_down)):
        @pl.when(inside)
        def _(copy=copy):
            copy.wait_recv()

        @pl.when(jnp.logical_not(inside))
        def _(ref=ref):
            ref[0:tiles] = jnp.zeros((tiles, 16, width), BF16)

        ref[tiles : 2 * tiles] = ref[0:tiles]

    def outer(a, carry):
        first = pl.multiple_of(a * ROWS, 16)
        for h, ref in enumerate((north, south)):
            pieces = windows(b_ref, ref, 2 * h, 2 * h, a)
            basis = jnp.dot(tab[2 * h, :, 4 * WIN :], jnp.concatenate(pieces, axis=0), preferred_element_type=F32)
            keep(2 * h, first, basis + part[h, a])
        return carry

    lax.fori_loop(0, lon // ROWS, outer, 0)
    s0 = mix_cycle(0)
    s2 = mix_cycle(2)
    three = [s.reshape(devices, 8, width) for s in (s0, spec1[...], s2)]
    three.append(jnp.zeros_like(three[0]))
    x_ref[...] = jnp.concatenate(three, axis=1).astype(BF16)

    def remote(src, dst, ssem, rsem, s, to, row):
        return pltpu.make_async_remote_copy(
            src_ref=src.at[to], dst_ref=dst.at[row], send_sem=ssem.at[s], recv_sem=rsem.at[row],
            device_id={"lat": to}, device_id_type=MESH,
        )

    def start_all(src, dst, ssem, rsem):
        def one(s, carry):
            remote(src, dst, ssem, rsem, s, lax.rem(me + s, devices), me).start()
            return carry

        lax.fori_loop(1, devices, one, 0)
        dst[me] = src[me]

    def wait_all(src, dst, ssem, rsem, send):
        def one(s, carry):
            peer = lax.rem(me + s, devices)
            copy = remote(src, dst, ssem, rsem, s, peer, peer)
            if send:
                copy.wait_send()
            else:
                copy.wait_recv()
            return carry

        lax.fori_loop(1, devices, one, 0)

    start_all(x_ref, recv, send_a, recv_a)

    @pl.when(me < devices - 1)
    def _():
        send_up.wait_send()

    @pl.when(me > 0)
    def _():
        send_down.wait_send()

    wait_all(x_ref, recv, send_a, recv_a, False)

    rows = 16 * BLK

    def chunk(ch, carry):
        for c in load(ch):
            c.wait()
        data = recv[...].reshape(devices * BLK, width)
        coef = jnp.dot(ana[...], data, preferred_element_type=F32)
        gain = gain_ref[pl.ds(pl.multiple_of(ch * CHUNK, CHUNK), CHUNK), :]
        gain = jnp.concatenate([gain] * M_DEV, axis=0)
        scaled = jnp.concatenate([coef[:half] * gain, coef[half:] * gain], axis=1).astype(BF16)
        mixed = jnp.dot(scaled, wide[...], preferred_element_type=F32).astype(BF16)
        stacked = jnp.concatenate([mixed[:, :width], mixed[:, width:]], axis=0)

        def piece(r, inner_carry):
            at = pl.ds(pl.multiple_of(r * rows, rows), rows)
            acc[at, :] += jnp.dot(syn[at, :], stacked, preferred_element_type=F32)
            return inner_carry

        lax.fori_loop(0, devices * BLK // rows, piece, 0)

        @pl.when(ch + 1 < chunks)
        def _():
            for c in load(ch + 1):
                c.start()

        return carry

    lax.fori_loop(0, chunks, chunk, 0)
    back[...] = acc[...].reshape(devices, BLK, width).astype(BF16)
    start_all(back, ret, send_b, recv_b)
    wait_all(x_ref, recv, send_a, recv_a, True)
    wait_all(back, ret, send_b, recv_b, False)
    got = ret[...].astype(F32)
    for i in range(3):
        out_ref[i] = got[:, 8 * i : 8 * i + 8, :].reshape(devices * 8, width).astype(BF16)
    wait_all(back, ret, send_b, recv_b, True)


def final_kernel(local_ref, modes_ref, inv_ref, out_ref):
    part = jnp.dot(inv_ref[...], modes_ref[0], preferred_element_type=F32)
    out_ref[0] = jax.nn.gelu(local_ref[0].astype(F32) + part).astype(BF16)


def body(devices, fwd_np, inv_np, leg_np, state, filters, blocks, mix, gain, weight):
    cycles, lon, ch = state.shape
    lat_count = cycles * devices
    fwd, inv = jnp.asarray(fwd_np), jnp.asarray(inv_np)
    if leg_np is not None:
        ana, syn = jnp.asarray(leg_np[0]), jnp.asarray(leg_np[1])
    else:
        own = lax.axis_index("lat") * M_DEV + jnp.arange(M_DEV, dtype=jnp.int32)
        theta = (jnp.arange(lat_count, dtype=F32) + 0.5) * (math.pi / lat_count)
        quad = jnp.sin(theta) * (2.0 * math.pi * math.pi / lat_count)
        ana, syn = spread(jnp, legendre_table(own, lat_count, lat_count), quad, devices)
        ana, syn = ana.astype(BF16)[None], syn.astype(BF16)[None]

    vmem = pl.BlockSpec(memory_space=pltpu.VMEM)
    smem = pl.BlockSpec(memory_space=pltpu.SMEM)
    hbm = pl.BlockSpec(memory_space=pl.ANY)
    shape = jax.ShapeDtypeStruct
    params = functools.partial(pltpu.CompilerParams, vmem_limit_bytes=48 * 2**20)
    block = pltpu.VMEM((devices, BLK, ch), BF16)
    cycle = pltpu.VMEM((lon // 8, 16, ch), BF16)
    rows = 2 * M_DEV * CHUNK
    sems = pltpu.SemaphoreType.DMA((devices,))
    turned = jnp.transpose(blocks, (0, 2, 1))
    local, modes = pl.pallas_call(
        functools.partial(main_kernel, devices),
        out_shape=(shape((cycles, lon, ch), BF16), shape((3, devices * 8, ch), BF16)),
        in_specs=[smem, smem, smem, hbm, vmem, vmem, hbm, hbm, vmem, vmem],
        out_specs=(vmem, vmem),
        scratch_shapes=[
            cycle, cycle, cycle, cycle, cycle,
            pltpu.VMEM((3, KB * ROWS, 6 * WIN), BF16),
            pltpu.VMEM((3, lon, KB * ch), BF16),
            pltpu.VMEM((2, lon // ROWS, KB * ROWS, ch), F32),
            pltpu.VMEM((devices * 8, ch), F32),
            block, block, block, block,
            pltpu.VMEM((rows, devices * BLK), BF16),
            pltpu.VMEM((devices * BLK, rows), BF16),
            pltpu.VMEM((2 * ch, 2 * ch), BF16),
            pltpu.VMEM((devices * BLK, ch), F32),
            pltpu.SemaphoreType.DMA((2,)),
            pltpu.SemaphoreType.DMA((6,)),
            pltpu.SemaphoreType.DMA((2,)),
            pltpu.SemaphoreType.DMA((2,)),
            sems, sems, sems, sems,
        ],
        compiler_params=params(collective_id=0, has_side_effects=True),
        name="main",
    )(
        jnp.transpose(filters, (0, 1, 4, 2, 3)), lon // 16 - 1 - turned // 2, 16 - 8 * (turned % 2),
        state.reshape(cycles, lon // 16, 16, ch), mix, fwd, ana, syn, gain, weight,
    )
    step = 480
    return pl.pallas_call(
        final_kernel,
        grid=(3, lon // step),
        out_shape=shape((cycles, lon, ch), BF16),
        in_specs=[
            pl.BlockSpec((1, step, ch), lambda i, n: (i, n, 0)),
            pl.BlockSpec((1, devices * 8, ch), lambda i, n: (i, 0, 0)),
            pl.BlockSpec((step, devices * 8), lambda i, n: (n, 0)),
        ],
        out_specs=pl.BlockSpec((1, step, ch), lambda i, n: (i, n, 0)),
        compiler_params=params(),
        name="final",
    )(local, modes, inv)


def solution(mesh):
    devices = mesh.shape["lat"]
    lon = 1440
    fwd, inv = constants(devices, lon)
    count = M_DEV * devices
    leg = None
    if count <= 96:
        table = legendre_np(count)
        quad = np.sin((np.arange(count) + 0.5) * (math.pi / count)) * (2.0 * math.pi**2 / count)
        pairs = [spread(np, table[M_DEV * d : M_DEV * d + M_DEV], quad, devices) for d in range(devices)]
        leg = [np.stack([p[n] for p in pairs]).astype(np.float32).astype(ml_dtypes.bfloat16) for n in range(2)]
    return jax.shard_map(
        functools.partial(body, devices, fwd, inv, leg),
        mesh=mesh,
        in_specs=(
            P(("groups", "lat"), None, None),
            P("lat", None, None, None, None),
            P("lat", None, None),
            P(),
            P(),
            P(),
        ),
        out_specs=P(("groups", "lat"), None, None),
        check_vma=False,
    )
```

```python
import functools
import math

import jax
import jax.numpy as jnp
import ml_dtypes
import numpy as np
from jax import lax
from jax.experimental import pallas as pl
from jax.experimental.pallas import tpu as pltpu
from jax.sharding import PartitionSpec as P

M_DEV = 3
KB = 3
SB = 8
ROWS = 48
WIN = 64
CHUNK = 48
BLK = 32
log_cut = -69.0
MESH = pl.DeviceIdType.MESH
F32 = jnp.float32
BF16 = jnp.bfloat16


def legendre_np(count):
    theta = (np.arange(count) + 0.5) * (math.pi / count)
    cosine, sine = np.cos(theta)[None], np.sin(theta)[None]
    m = np.arange(count, dtype=np.float64)[:, None]
    lg = np.array([math.lgamma(x + 0.5) - math.lgamma(x + 1.0) for x in range(count)])[:, None]
    g = 0.5 * (np.log(2 * m + 1) - math.log(4 * math.pi)) + 0.5 * (lg - 0.5 * math.log(math.pi)) + m * np.log(sine)
    first = np.where(g < log_cut, 0.0, np.exp(g))
    table = np.zeros((count, count, count))
    before = current = np.zeros((count, count))
    for l in range(count):
        up = np.sqrt((4.0 * l * l - 1.0) / np.maximum(l * l - m * m, 1.0)) if l else 0.0 * m
        down = np.sqrt(np.maximum((l - 1.0) ** 2 - m * m, 0.0) / max(4.0 * (l - 1.0) ** 2 - 1.0, 1.0))
        general = up * (cosine * current - down * before)
        second = np.sqrt(2 * m + 3) * cosine * current
        value = np.where(l < m, 0.0, np.where(l == m, first, np.where(l == m + 1, second, general)))
        before, current = current, value
        table[:, l] = value
    return table


def legendre_table(wave_orders, degree_count, lat_count):
    colatitude = (jnp.arange(lat_count, dtype=F32) + 0.5) * (math.pi / lat_count)
    cosine = jnp.cos(colatitude)[None, :]
    sine_col = jnp.sin(colatitude)[None, :]
    orders = wave_orders.astype(F32)[:, None]
    log_first = (
        0.5 * (jnp.log(2.0 * orders + 1.0) - math.log(4.0 * math.pi))
        + 0.5 * (lax.lgamma(orders + 0.5) - 0.5 * math.log(math.pi) - lax.lgamma(orders + 1.0))
        + orders * jnp.log(sine_col)
    )
    first_term = jnp.where(log_first < log_cut, 0.0, jnp.exp(log_first))

    def advance(state_pair, degree):
        before, current = state_pair
        deg_sq = degree * degree
        ord_sq = orders * orders
        lower_deg = degree - 1.0
        coef_up = jnp.sqrt(jnp.maximum(4.0 * deg_sq - 1.0, 0.0) / jnp.maximum(deg_sq - ord_sq, 1.0))
        coef_down = jnp.sqrt(
            jnp.maximum(lower_deg * lower_deg - ord_sq, 0.0)
            / jnp.maximum(4.0 * lower_deg * lower_deg - 1.0, 1.0)
        )
        general = coef_up * (cosine * current - coef_down * before)
        second = jnp.sqrt(2.0 * orders + 3.0) * cosine * current
        next_value = jnp.where(
            degree < orders,
            0.0,
            jnp.where(
                degree == orders, first_term, jnp.where(degree == orders + 1.0, second, general)
            ),
        )
        return ((current, next_value), next_value)

    zeros_state = jnp.zeros((orders.shape[0], lat_count), F32)
    degrees = jnp.arange(degree_count, dtype=F32)
    _, table_rows = lax.scan(advance, (zeros_state, zeros_state), degrees)
    return jnp.transpose(table_rows, (1, 0, 2))


def spread(xp, table, quad, devices):
    count = table.shape[1]
    chunks = count // CHUNK
    lat = xp.arange(count)[:, None]
    col = xp.arange(devices * BLK)[None, :]
    here = (lat == 3 * (col // BLK) + col % BLK // 8) & (col % BLK < 24)
    per = devices * 16
    late = col // per
    source = xp.where(late == 0, 1, 2 * (col % 16 // 8))
    there = (lat == 3 * (col % per // 16) + source) & ((late == 1) | (col % 16 < 8))

    def lay(values, here):
        if xp is jnp:
            values = values.astype(BF16)
        rows = []
        for p in range(2):
            for m in range(M_DEV):
                pick = (here & (col % 8 == 2 * m + p)).astype(values.dtype)
                rows.append(xp.matmul(values[m], pick).reshape(chunks, 1, CHUNK, devices * BLK))
        return xp.concatenate(rows, axis=1).reshape(chunks, 2 * M_DEV * CHUNK, devices * BLK)

    return lay(table * quad[None, None, :], there), lay(table, here).transpose(0, 2, 1)


def constants(devices, lon):
    modes = M_DEV * devices
    angle = (np.arange(modes)[:, None] * np.arange(lon)[None, :] % lon) * (2.0 * math.pi / lon)
    factor = np.where(np.arange(modes) == 0, 1.0, 2.0)[:, None]

    def pad(re, im):
        paired = np.stack([re, im], axis=1).reshape(devices, 2 * M_DEV, lon)
        return np.pad(paired, ((0, 0), (0, 2), (0, 0))).reshape(devices * 8, lon)

    bf = ml_dtypes.bfloat16
    fwd = pad(np.cos(angle) / lon, -np.sin(angle) / lon).astype(np.float32).astype(bf)
    inv = pad(factor * np.cos(angle), -factor * np.sin(angle)).T.astype(np.float32).astype(bf)
    return fwd, inv


def fill_toeplitz(t_ref, f_ref, o_ref, cycle, offset, column):
    shape = (ROWS, 2 * WIN)
    lane = lax.broadcasted_iota(jnp.int32, shape, 1)
    first_slot = lane < WIN
    off = [o_ref[cycle, slot, offset] for slot in range(2)]
    delta = (
        lax.broadcasted_iota(jnp.int32, shape, 0)
        + jnp.where(first_slot, off[0], off[1] + WIN)
        - lane
    )
    parts = [jnp.zeros(shape, F32) for _ in range(KB)]
    for t in range(SB):
        hit = delta == t
        for k in range(KB):
            value = jnp.where(first_slot, f_ref[cycle, offset, k, 0, t], f_ref[cycle, offset, k, 1, t])
            parts[k] = jnp.where(hit, value, parts[k])
    for k in range(KB):
        t_ref[cycle, k * ROWS : (k + 1) * ROWS, column * 2 * WIN : (column + 1) * 2 * WIN] = parts[k].astype(BF16)


def windows(b_ref, ref, cycle, offset, a):
    pieces = []
    for slot in range(2):
        row = b_ref[cycle, slot, offset] + a * (ROWS // 16)
        pieces += [ref[row + n] for n in range(WIN // 16)]
    return pieces


def main_kernel(
    devices, f_ref, b_ref, o_ref, x_hbm, mix_hbm, fwd_hbm, ana_hbm, syn_hbm, gain_hbm, w_hbm,
    loc_hbm, out_ref,
    loc_ref, mix_ref, fwd_ref, gain_ref, w_ref, own_sem, loc_sem,
    e0, e1, e2, north, south, tab, bas, part,
    x_mid, x_ref, recv_mid, recv, back, ret, ana, syn, wide, acc,
    load_sem, x_sem, halo_send, halo_recv, send_a, recv_a, send_b, recv_b, send_c, recv_c,
):
    me = lax.axis_index("lat")
    tiles = x_hbm.shape[1]
    lon = tiles * 16
    chunks = ana_hbm.shape[1]
    mine = me if ana_hbm.shape[0] > 1 else 0
    width = w_ref.shape[2]
    half = M_DEV * CHUNK

    barrier = pltpu.get_barrier_semaphore()

    def greet(s, carry):
        pl.semaphore_signal(barrier, inc=1, device_id={"lat": lax.rem(me + s, devices)}, device_id_type=MESH)
        return carry

    lax.fori_loop(1, devices, greet, 0)

    held = (e0, e1, e2)
    fetches = []
    for i in range(3):
        fetches.append(pltpu.make_async_copy(x_hbm.at[i], held[i].at[pl.ds(0, tiles)], x_sem.at[2 * i]))
        fetches.append(
            pltpu.make_async_copy(x_hbm.at[i], held[i].at[pl.ds(tiles, tiles)], x_sem.at[2 * i + 1])
        )
    for c in fetches:
        c.start()
    small = [
        pltpu.make_async_copy(src, dst, own_sem.at[n])
        for n, (src, dst) in enumerate(
            ((w_hbm, w_ref), (mix_hbm, mix_ref), (fwd_hbm, fwd_ref), (gain_hbm, gain_ref))
        )
    ]
    for c in small:
        c.start()

    def load(ch):
        return (
            pltpu.make_async_copy(ana_hbm.at[mine, ch], ana, load_sem.at[0]),
            pltpu.make_async_copy(syn_hbm.at[mine, ch], syn, load_sem.at[1]),
        )

    for c in load(0):
        c.start()
    pl.semaphore_wait(barrier, devices - 1)

    send_up = pltpu.make_async_remote_copy(
        src_ref=x_hbm.at[2], dst_ref=north.at[pl.ds(0, tiles)], send_sem=halo_send.at[0], recv_sem=halo_recv.at[0],
        device_id={"lat": lax.rem(me + 1, devices)}, device_id_type=MESH,
    )
    send_down = pltpu.make_async_remote_copy(
        src_ref=x_hbm.at[0], dst_ref=south.at[pl.ds(0, tiles)], send_sem=halo_send.at[1], recv_sem=halo_recv.at[1],
        device_id={"lat": lax.rem(me + devices - 1, devices)}, device_id_type=MESH,
    )

    @pl.when(me < devices - 1)
    def _():
        send_up.start()

    @pl.when(me > 0)
    def _():
        send_down.start()

    plan = {0: ((0, 1), (1, 2)), 1: ((0, 0), (1, 1), (2, 2)), 2: ((1, 0), (2, 1))}
    for i in range(3):
        for n, (_, offset) in enumerate(plan[i]):
            fill_toeplitz(tab, f_ref, o_ref, i, offset, n)
    fill_toeplitz(tab, f_ref, o_ref, 0, 0, 2)
    fill_toeplitz(tab, f_ref, o_ref, 2, 2, 2)
    for c in small:
        c.wait()
    wide[0:width, 0:width] = w_ref[0]
    wide[0:width, width:] = w_ref[1]
    wide[width:, 0:width] = -w_ref[1]
    wide[width:, width:] = w_ref[0]
    acc[...] = jnp.zeros_like(acc)
    for c in fetches:
        c.wait()

    def keep(i, first, basis):
        basis = basis.astype(BF16)
        for k in range(KB):
            bas[i, pl.ds(first, ROWS), k * width : (k + 1) * width] = basis[k * ROWS : (k + 1) * ROWS]

    def inner(a, carry):
        first = pl.multiple_of(a * ROWS, 16)
        for i in range(3):
            pieces = []
            for source, offset in plan[i]:
                pieces += windows(b_ref, held[source], i, offset, a)
            used = len(pieces) * 16
            basis = jnp.dot(tab[i, :, 0:used], jnp.concatenate(pieces, axis=0), preferred_element_type=F32)
            if i == 1:
                keep(i, first, basis)
            else:
                part[i // 2, a] = basis
        return carry

    lax.fori_loop(0, lon // ROWS, inner, 0)

    def remote(src, dst, ssem, rsem, s, to, row):
        return pltpu.make_async_remote_copy(
            src_ref=src.at[to], dst_ref=dst.at[row], send_sem=ssem.at[s], recv_sem=rsem.at[row],
            device_id={"lat": to}, device_id_type=MESH,
        )

    def start_all(src, dst, ssem, rsem):
        def one(s, carry):
            remote(src, dst, ssem, rsem, s, lax.rem(me + s, devices), me).start()
            return carry

        lax.fori_loop(1, devices, one, 0)
        dst[me] = src[me]

    def wait_all(src, dst, ssem, rsem, send):
        def one(s, carry):
            peer = lax.rem(me + s, devices)
            copy = remote(src, dst, ssem, rsem, s, peer, peer)
            if send:
                copy.wait_send()
            else:
                copy.wait_recv()
            return carry

        lax.fori_loop(1, devices, one, 0)

    step = lon // 3

    leave = [pltpu.make_async_copy(loc_ref.at[i], loc_hbm.at[i], loc_sem.at[i]) for i in range(3)]

    def mix_cycle(i):
        def one(n, carry):
            at = pl.ds(pl.multiple_of(n * step, 16), step)
            loc_ref[i, at, :] = jnp.dot(bas[i, at, :], mix_ref[...], preferred_element_type=F32).astype(BF16)
            return carry

        lax.fori_loop(0, 3, one, 0)
        leave[i].start()
        return jnp.dot(fwd_ref[...], loc_ref[i], preferred_element_type=F32)

    mid = mix_cycle(1).reshape(devices, 8, width)
    x_mid[...] = jnp.concatenate([mid, jnp.zeros_like(mid)], axis=1).astype(BF16)
    start_all(x_mid, recv_mid, send_c, recv_c)

    for ref, inside, copy in ((north, me > 0, send_up), (south, me < devices - 1, send_down)):
        @pl.when(inside)
        def _(copy=copy):
            copy.wait_recv()

        @pl.when(jnp.logical_not(inside))
        def _(ref=ref):
            ref[0:tiles] = jnp.zeros((tiles, 16, width), BF16)

        ref[tiles : 2 * tiles] = ref[0:tiles]

    def outer(a, carry):
        first = pl.multiple_of(a * ROWS, 16)
        for h, ref in enumerate((north, south)):
            pieces = windows(b_ref, ref, 2 * h, 2 * h, a)
            basis = jnp.dot(tab[2 * h, :, 4 * WIN :], jnp.concatenate(pieces, axis=0), preferred_element_type=F32)
            keep(2 * h, first, basis + part[h, a])
        return carry

    lax.fori_loop(0, lon // ROWS, outer, 0)
    s0 = mix_cycle(0)
    s2 = mix_cycle(2)
    pair = [s.reshape(devices, 8, width) for s in (s0, s2)]
    x_ref[...] = jnp.concatenate(pair, axis=1).astype(BF16)
    start_all(x_ref, recv, send_a, recv_a)

    @pl.when(me < devices - 1)
    def _():
        send_up.wait_send()

    @pl.when(me > 0)
    def _():
        send_down.wait_send()

    wait_all(x_mid, recv_mid, send_c, recv_c, False)
    wait_all(x_ref, recv, send_a, recv_a, False)

    rows = 16 * BLK

    def chunk(ch, carry):
        for c in load(ch):
            c.wait()
        data = jnp.concatenate(
            [ref[...].reshape(devices * 16, width) for ref in (recv_mid, recv)], axis=0
        )
        coef = jnp.dot(ana[...], data, preferred_element_type=F32)
        gain = gain_ref[pl.ds(pl.multiple_of(ch * CHUNK, CHUNK), CHUNK), :]
        gain = jnp.concatenate([gain] * M_DEV, axis=0)
        scaled = jnp.concatenate([coef[:half] * gain, coef[half:] * gain], axis=1).astype(BF16)
        mixed = jnp.dot(scaled, wide[...], preferred_element_type=F32).astype(BF16)
        stacked = jnp.concatenate([mixed[:, :width], mixed[:, width:]], axis=0)

        def piece(r, inner_carry):
            at = pl.ds(pl.multiple_of(r * rows, rows), rows)
            acc[at, :] += jnp.dot(syn[at, :], stacked, preferred_element_type=F32)
            return inner_carry

        lax.fori_loop(0, devices * BLK // rows, piece, 0)

        @pl.when(ch + 1 < chunks)
        def _():
            for c in load(ch + 1):
                c.start()

        return carry

    lax.fori_loop(0, chunks, chunk, 0)
    back[...] = acc[...].reshape(devices, BLK, width).astype(BF16)
    start_all(back, ret, send_b, recv_b)
    wait_all(x_mid, recv_mid, send_c, recv_c, True)
    wait_all(x_ref, recv, send_a, recv_a, True)
    for c in leave:
        c.wait()
    wait_all(back, ret, send_b, recv_b, False)
    got = ret[...].astype(F32)
    for i in range(3):
        out_ref[i] = got[:, 8 * i : 8 * i + 8, :].reshape(devices * 8, width).astype(BF16)
    wait_all(back, ret, send_b, recv_b, True)


def final_kernel(local_ref, modes_ref, inv_ref, out_ref):
    part = jnp.dot(inv_ref[...], modes_ref[0], preferred_element_type=F32)
    out_ref[0] = jax.nn.gelu(local_ref[0].astype(F32) + part).astype(BF16)


def body(devices, fwd_np, inv_np, leg_np, state, filters, blocks, mix, gain, weight):
    cycles, lon, ch = state.shape
    lat_count = cycles * devices
    fwd, inv = jnp.asarray(fwd_np), jnp.asarray(inv_np)
    if leg_np is not None:
        ana, syn = jnp.asarray(leg_np[0]), jnp.asarray(leg_np[1])
    else:
        own = lax.axis_index("lat") * M_DEV + jnp.arange(M_DEV, dtype=jnp.int32)
        theta = (jnp.arange(lat_count, dtype=F32) + 0.5) * (math.pi / lat_count)
        quad = jnp.sin(theta) * (2.0 * math.pi * math.pi / lat_count)
        ana, syn = spread(jnp, legendre_table(own, lat_count, lat_count), quad, devices)
        ana, syn = ana.astype(BF16)[None], syn.astype(BF16)[None]

    vmem = pl.BlockSpec(memory_space=pltpu.VMEM)
    smem = pl.BlockSpec(memory_space=pltpu.SMEM)
    hbm = pl.BlockSpec(memory_space=pl.ANY)
    shape = jax.ShapeDtypeStruct
    params = functools.partial(pltpu.CompilerParams, vmem_limit_bytes=48 * 2**20)
    block = pltpu.VMEM((devices, BLK, ch), BF16)
    thin = pltpu.VMEM((devices, 16, ch), BF16)
    cycle = pltpu.VMEM((lon // 8, 16, ch), BF16)
    rows = 2 * M_DEV * CHUNK
    sems = pltpu.SemaphoreType.DMA((devices,))
    turned = jnp.transpose(blocks, (0, 2, 1))
    local, modes = pl.pallas_call(
        functools.partial(main_kernel, devices),
        out_shape=(shape((cycles, lon, ch), BF16), shape((3, devices * 8, ch), BF16)),
        in_specs=[smem, smem, smem] + [hbm] * 7,
        out_specs=(hbm, vmem),
        scratch_shapes=[
            pltpu.VMEM((cycles, lon, ch), BF16),
            pltpu.VMEM(mix.shape, BF16),
            pltpu.VMEM(fwd.shape, BF16),
            pltpu.VMEM(gain.shape, F32),
            pltpu.VMEM(weight.shape, BF16),
            pltpu.SemaphoreType.DMA((4,)),
            pltpu.SemaphoreType.DMA((3,)),
            cycle, cycle, cycle, cycle, cycle,
            pltpu.VMEM((3, KB * ROWS, 6 * WIN), BF16),
            pltpu.VMEM((3, lon, KB * ch), BF16),
            pltpu.VMEM((2, lon // ROWS, KB * ROWS, ch), F32),
            thin, thin, thin, thin, block, block,
            pltpu.VMEM((rows, devices * BLK), BF16),
            pltpu.VMEM((devices * BLK, rows), BF16),
            pltpu.VMEM((2 * ch, 2 * ch), BF16),
            pltpu.VMEM((devices * BLK, ch), F32),
            pltpu.SemaphoreType.DMA((2,)),
            pltpu.SemaphoreType.DMA((6,)),
            pltpu.SemaphoreType.DMA((2,)),
            pltpu.SemaphoreType.DMA((2,)),
            sems, sems, sems, sems, sems, sems,
        ],
        compiler_params=pltpu.CompilerParams(
            vmem_limit_bytes=60 * 2**20, collective_id=0, has_side_effects=True
        ),
        name="main",
    )(
        jnp.transpose(filters, (0, 1, 4, 2, 3)), lon // 16 - 1 - turned // 2, 16 - 8 * (turned % 2),
        state.reshape(cycles, lon // 16, 16, ch), mix, fwd, ana, syn, gain, weight,
    )
    step = 480
    return pl.pallas_call(
        final_kernel,
        grid=(3, lon // step),
        out_shape=shape((cycles, lon, ch), BF16),
        in_specs=[
            pl.BlockSpec((1, step, ch), lambda i, n: (i, n, 0)),
            pl.BlockSpec((1, devices * 8, ch), lambda i, n: (i, 0, 0)),
            pl.BlockSpec((step, devices * 8), lambda i, n: (n, 0)),
        ],
        out_specs=pl.BlockSpec((1, step, ch), lambda i, n: (i, n, 0)),
        compiler_params=params(),
        name="final",
    )(local, modes, inv)


def solution(mesh):
    devices = mesh.shape["lat"]
    lon = 1440
    fwd, inv = constants(devices, lon)
    count = M_DEV * devices
    leg = None
    if count <= 96:
        table = legendre_np(count)
        quad = np.sin((np.arange(count) + 0.5) * (math.pi / count)) * (2.0 * math.pi**2 / count)
        pairs = [spread(np, table[M_DEV * d : M_DEV * d + M_DEV], quad, devices) for d in range(devices)]
        leg = [np.stack([p[n] for p in pairs]).astype(np.float32).astype(ml_dtypes.bfloat16) for n in range(2)]
    return jax.shard_map(
        functools.partial(body, devices, fwd, inv, leg),
        mesh=mesh,
        in_specs=(
            P(("groups", "lat"), None, None),
            P("lat", None, None, None, None),
            P("lat", None, None),
            P(),
            P(),
            P(),
        ),
        out_specs=P(("groups", "lat"), None, None),
        check_vma=False,
    )
```

```python
import functools
import math

import jax
import jax.numpy as jnp
import ml_dtypes
import numpy as np
from jax import lax
from jax.experimental import pallas as pl
from jax.experimental.pallas import tpu as pltpu
from jax.sharding import PartitionSpec as P

M_DEV = 3
KB = 3
SB = 8
ROWS = 48
WIN = 64
CHUNK = 48
BLK = 32
log_cut = -69.0
MESH = pl.DeviceIdType.MESH
F32 = jnp.float32
BF16 = jnp.bfloat16


def legendre_np(count):
    theta = (np.arange(count) + 0.5) * (math.pi / count)
    cosine, sine = np.cos(theta)[None], np.sin(theta)[None]
    m = np.arange(count, dtype=np.float64)[:, None]
    lg = np.array([math.lgamma(x + 0.5) - math.lgamma(x + 1.0) for x in range(count)])[:, None]
    g = 0.5 * (np.log(2 * m + 1) - math.log(4 * math.pi)) + 0.5 * (lg - 0.5 * math.log(math.pi)) + m * np.log(sine)
    first = np.where(g < log_cut, 0.0, np.exp(g))
    table = np.zeros((count, count, count))
    before = current = np.zeros((count, count))
    for l in range(count):
        up = np.sqrt((4.0 * l * l - 1.0) / np.maximum(l * l - m * m, 1.0)) if l else 0.0 * m
        down = np.sqrt(np.maximum((l - 1.0) ** 2 - m * m, 0.0) / max(4.0 * (l - 1.0) ** 2 - 1.0, 1.0))
        general = up * (cosine * current - down * before)
        second = np.sqrt(2 * m + 3) * cosine * current
        value = np.where(l < m, 0.0, np.where(l == m, first, np.where(l == m + 1, second, general)))
        before, current = current, value
        table[:, l] = value
    return table


def legendre_table(wave_orders, degree_count, lat_count):
    colatitude = (jnp.arange(lat_count, dtype=F32) + 0.5) * (math.pi / lat_count)
    cosine = jnp.cos(colatitude)[None, :]
    sine_col = jnp.sin(colatitude)[None, :]
    orders = wave_orders.astype(F32)[:, None]
    log_first = (
        0.5 * (jnp.log(2.0 * orders + 1.0) - math.log(4.0 * math.pi))
        + 0.5 * (lax.lgamma(orders + 0.5) - 0.5 * math.log(math.pi) - lax.lgamma(orders + 1.0))
        + orders * jnp.log(sine_col)
    )
    first_term = jnp.where(log_first < log_cut, 0.0, jnp.exp(log_first))

    def advance(state_pair, degree):
        before, current = state_pair
        deg_sq = degree * degree
        ord_sq = orders * orders
        lower_deg = degree - 1.0
        coef_up = jnp.sqrt(jnp.maximum(4.0 * deg_sq - 1.0, 0.0) / jnp.maximum(deg_sq - ord_sq, 1.0))
        coef_down = jnp.sqrt(
            jnp.maximum(lower_deg * lower_deg - ord_sq, 0.0)
            / jnp.maximum(4.0 * lower_deg * lower_deg - 1.0, 1.0)
        )
        general = coef_up * (cosine * current - coef_down * before)
        second = jnp.sqrt(2.0 * orders + 3.0) * cosine * current
        next_value = jnp.where(
            degree < orders,
            0.0,
            jnp.where(
                degree == orders, first_term, jnp.where(degree == orders + 1.0, second, general)
            ),
        )
        return ((current, next_value), next_value)

    zeros_state = jnp.zeros((orders.shape[0], lat_count), F32)
    degrees = jnp.arange(degree_count, dtype=F32)
    _, table_rows = lax.scan(advance, (zeros_state, zeros_state), degrees)
    return jnp.transpose(table_rows, (1, 0, 2))


def spread(xp, table, quad, devices):
    count = table.shape[1]
    chunks = count // CHUNK
    lat = xp.arange(count)[:, None]
    col = xp.arange(devices * BLK)[None, :]
    here = (lat == 3 * (col // BLK) + col % BLK // 8) & (col % BLK < 24)
    per = devices * 16
    late = col // per
    source = xp.where(late == 0, 1, 2 * (col % 16 // 8))
    there = (lat == 3 * (col % per // 16) + source) & ((late == 1) | (col % 16 < 8))

    def lay(values, here):
        if xp is jnp:
            values = values.astype(BF16)
        rows = []
        for p in range(2):
            for m in range(M_DEV):
                pick = (here & (col % 8 == 2 * m + p)).astype(values.dtype)
                rows.append(xp.matmul(values[m], pick).reshape(chunks, 1, CHUNK, devices * BLK))
        return xp.concatenate(rows, axis=1).reshape(chunks, 2 * M_DEV * CHUNK, devices * BLK)

    return lay(table * quad[None, None, :], there), lay(table, here).transpose(0, 2, 1)


def constants(devices, lon):
    modes = M_DEV * devices
    angle = (np.arange(modes)[:, None] * np.arange(lon)[None, :] % lon) * (2.0 * math.pi / lon)
    factor = np.where(np.arange(modes) == 0, 1.0, 2.0)[:, None]

    def pad(re, im):
        paired = np.stack([re, im], axis=1).reshape(devices, 2 * M_DEV, lon)
        return np.pad(paired, ((0, 0), (0, 2), (0, 0))).reshape(devices * 8, lon)

    bf = ml_dtypes.bfloat16
    fwd = pad(np.cos(angle) / lon, -np.sin(angle) / lon).astype(np.float32).astype(bf)
    inv = pad(factor * np.cos(angle), -factor * np.sin(angle)).T.astype(np.float32).astype(bf)
    return fwd, inv


def fill_toeplitz(t_ref, f_ref, o_ref, cycle, offset, column):
    shape = (ROWS, 2 * WIN)
    lane = lax.broadcasted_iota(jnp.int32, shape, 1)
    first_slot = lane < WIN
    off = [o_ref[cycle, slot, offset] for slot in range(2)]
    delta = (
        lax.broadcasted_iota(jnp.int32, shape, 0)
        + jnp.where(first_slot, off[0], off[1] + WIN)
        - lane
    )
    parts = [jnp.zeros(shape, F32) for _ in range(KB)]
    for t in range(SB):
        hit = delta == t
        for k in range(KB):
            value = jnp.where(first_slot, f_ref[cycle, offset, k, 0, t], f_ref[cycle, offset, k, 1, t])
            parts[k] = jnp.where(hit, value, parts[k])
    for k in range(KB):
        t_ref[cycle, k * ROWS : (k + 1) * ROWS, column * 2 * WIN : (column + 1) * 2 * WIN] = parts[k].astype(BF16)


def windows(b_ref, ref, cycle, offset, a):
    pieces = []
    for slot in range(2):
        row = b_ref[cycle, slot, offset] + a * (ROWS // 16)
        pieces += [ref[row + n] for n in range(WIN // 16)]
    return pieces


def main_kernel(
    devices, f_ref, b_ref, o_ref, x_hbm, mix_hbm, fwd_hbm, ana_hbm, syn_hbm, gain_hbm, w_hbm,
    loc_hbm, out_ref,
    loc_ref, mix_ref, fwd_ref, gain_ref, w_ref, own_sem, loc_sem,
    e0, e1, e2, north, south, tab, bas, part,
    x_mid, x_ref, recv_mid, recv, back, ret, ana, syn, wide, acc,
    load_sem, x_sem, halo_send, halo_recv, send_a, recv_a, send_b, recv_b, send_c, recv_c,
):
    me = lax.axis_index("lat")
    tiles = x_hbm.shape[1]
    lon = tiles * 16
    chunks = ana_hbm.shape[1]
    mine = me if ana_hbm.shape[0] > 1 else 0
    width = w_ref.shape[2]
    half = M_DEV * CHUNK

    barrier = pltpu.get_barrier_semaphore()

    def greet(s, carry):
        pl.semaphore_signal(barrier, inc=1, device_id={"lat": lax.rem(me + s, devices)}, device_id_type=MESH)
        return carry

    lax.fori_loop(1, devices, greet, 0)

    held = (e0, e1, e2)
    fetches = []
    for i in range(3):
        fetches.append(pltpu.make_async_copy(x_hbm.at[i], held[i].at[pl.ds(0, tiles)], x_sem.at[2 * i]))
        fetches.append(
            pltpu.make_async_copy(x_hbm.at[i], held[i].at[pl.ds(tiles, tiles)], x_sem.at[2 * i + 1])
        )
    for c in fetches:
        c.start()
    small = [
        pltpu.make_async_copy(src, dst, own_sem.at[n])
        for n, (src, dst) in enumerate(
            ((w_hbm, w_ref), (mix_hbm, mix_ref), (fwd_hbm, fwd_ref), (gain_hbm, gain_ref))
        )
    ]
    for c in small:
        c.start()

    def load(ch):
        return (
            pltpu.make_async_copy(ana_hbm.at[mine, ch], ana, load_sem.at[0]),
            pltpu.make_async_copy(syn_hbm.at[mine, ch], syn, load_sem.at[1]),
        )

    for c in load(0):
        c.start()
    pl.semaphore_wait(barrier, devices - 1)

    send_up = pltpu.make_async_remote_copy(
        src_ref=x_hbm.at[2], dst_ref=north.at[pl.ds(0, tiles)], send_sem=halo_send.at[0], recv_sem=halo_recv.at[0],
        device_id={"lat": lax.rem(me + 1, devices)}, device_id_type=MESH,
    )
    send_down = pltpu.make_async_remote_copy(
        src_ref=x_hbm.at[0], dst_ref=south.at[pl.ds(0, tiles)], send_sem=halo_send.at[1], recv_sem=halo_recv.at[1],
        device_id={"lat": lax.rem(me + devices - 1, devices)}, device_id_type=MESH,
    )

    @pl.when(me < devices - 1)
    def _():
        send_up.start()

    @pl.when(me > 0)
    def _():
        send_down.start()

    plan = {0: ((0, 1), (1, 2)), 1: ((0, 0), (1, 1), (2, 2)), 2: ((1, 0), (2, 1))}
    for i in range(3):
        for n, (_, offset) in enumerate(plan[i]):
            fill_toeplitz(tab, f_ref, o_ref, i, offset, n)
    fill_toeplitz(tab, f_ref, o_ref, 0, 0, 2)
    fill_toeplitz(tab, f_ref, o_ref, 2, 2, 2)
    for c in small:
        c.wait()
    wide[0:width, 0:width] = w_ref[0]
    wide[0:width, width:] = w_ref[1]
    wide[width:, 0:width] = -w_ref[1]
    wide[width:, width:] = w_ref[0]
    acc[...] = jnp.zeros_like(acc)
    for c in fetches:
        c.wait()

    def keep(i, first, basis):
        basis = basis.astype(BF16)
        for k in range(KB):
            bas[i, pl.ds(first, ROWS), k * width : (k + 1) * width] = basis[k * ROWS : (k + 1) * ROWS]

    def inner(a, carry):
        first = pl.multiple_of(a * ROWS, 16)
        for i in range(3):
            pieces = []
            for source, offset in plan[i]:
                pieces += windows(b_ref, held[source], i, offset, a)
            used = len(pieces) * 16
            basis = jnp.dot(tab[i, :, 0:used], jnp.concatenate(pieces, axis=0), preferred_element_type=F32)
            if i == 1:
                keep(i, first, basis)
            else:
                part[i // 2, a] = basis
        return carry

    lax.fori_loop(0, lon // ROWS, inner, 0)

    def remote(src, dst, ssem, rsem, s, to, row):
        return pltpu.make_async_remote_copy(
            src_ref=src.at[to], dst_ref=dst.at[row], send_sem=ssem.at[s], recv_sem=rsem.at[row],
            device_id={"lat": to}, device_id_type=MESH,
        )

    def start_all(src, dst, ssem, rsem):
        def one(s, carry):
            remote(src, dst, ssem, rsem, s, lax.rem(me + s, devices), me).start()
            return carry

        lax.fori_loop(1, devices, one, 0)
        dst[me] = src[me]

    def wait_all(src, dst, ssem, rsem, send):
        def one(s, carry):
            peer = lax.rem(me + s, devices)
            copy = remote(src, dst, ssem, rsem, s, peer, peer)
            if send:
                copy.wait_send()
            else:
                copy.wait_recv()
            return carry

        lax.fori_loop(1, devices, one, 0)

    step = lon // 3

    leave = [pltpu.make_async_copy(loc_ref.at[i], loc_hbm.at[i], loc_sem.at[i]) for i in range(3)]

    def mix_cycle(i):
        def one(n, carry):
            at = pl.ds(pl.multiple_of(n * step, 16), step)
            loc_ref[i, at, :] = jnp.dot(bas[i, at, :], mix_ref[...], preferred_element_type=F32).astype(BF16)
            return carry

        lax.fori_loop(0, 3, one, 0)
        leave[i].start()
        return jnp.dot(fwd_ref[...], loc_ref[i], preferred_element_type=F32)

    mid = mix_cycle(1).reshape(devices, 8, width)
    x_mid[...] = jnp.concatenate([mid, jnp.zeros_like(mid)], axis=1).astype(BF16)
    start_all(x_mid, recv_mid, send_c, recv_c)

    for ref, inside, copy in ((north, me > 0, send_up), (south, me < devices - 1, send_down)):
        @pl.when(inside)
        def _(copy=copy):
            copy.wait_recv()

        @pl.when(jnp.logical_not(inside))
        def _(ref=ref):
            ref[0:tiles] = jnp.zeros((tiles, 16, width), BF16)

        ref[tiles : 2 * tiles] = ref[0:tiles]

    def outer(group, carry):
        work = []
        for a in (3 * group, 3 * group + 1, 3 * group + 2):
            for h, ref in enumerate((north, south)):
                data = jnp.concatenate(windows(b_ref, ref, 2 * h, 2 * h, a), axis=0)
                basis = jnp.dot(tab[2 * h, :, 4 * WIN :], data, preferred_element_type=F32)
                work.append((h, a, basis + part[h, a]))
        for h, a, basis in work:
            keep(2 * h, pl.multiple_of(a * ROWS, 16), basis)
        return carry

    lax.fori_loop(0, lon // ROWS // 3, outer, 0)
    s0 = mix_cycle(0)
    s2 = mix_cycle(2)
    pair = [s.reshape(devices, 8, width) for s in (s0, s2)]
    x_ref[...] = jnp.concatenate(pair, axis=1).astype(BF16)
    start_all(x_ref, recv, send_a, recv_a)

    @pl.when(me < devices - 1)
    def _():
        send_up.wait_send()

    @pl.when(me > 0)
    def _():
        send_down.wait_send()

    wait_all(x_mid, recv_mid, send_c, recv_c, False)
    wait_all(x_ref, recv, send_a, recv_a, False)

    rows = 16 * BLK

    def chunk(ch, carry):
        for c in load(ch):
            c.wait()
        data = jnp.concatenate(
            [ref[...].reshape(devices * 16, width) for ref in (recv_mid, recv)], axis=0
        )
        coef = jnp.dot(ana[...], data, preferred_element_type=F32)
        gain = gain_ref[pl.ds(pl.multiple_of(ch * CHUNK, CHUNK), CHUNK), :]
        gain = jnp.concatenate([gain] * M_DEV, axis=0)
        scaled = jnp.concatenate([coef[:half] * gain, coef[half:] * gain], axis=1).astype(BF16)
        mixed = jnp.dot(scaled, wide[...], preferred_element_type=F32).astype(BF16)
        stacked = jnp.concatenate([mixed[:, :width], mixed[:, width:]], axis=0)

        def piece(r, inner_carry):
            at = pl.ds(pl.multiple_of(r * rows, rows), rows)
            acc[at, :] += jnp.dot(syn[at, :], stacked, preferred_element_type=F32)
            return inner_carry

        lax.fori_loop(0, devices * BLK // rows, piece, 0)

        @pl.when(ch + 1 < chunks)
        def _():
            for c in load(ch + 1):
                c.start()

        return carry

    lax.fori_loop(0, chunks, chunk, 0)
    back[...] = acc[...].reshape(devices, BLK, width).astype(BF16)
    start_all(back, ret, send_b, recv_b)
    wait_all(x_mid, recv_mid, send_c, recv_c, True)
    wait_all(x_ref, recv, send_a, recv_a, True)
    for c in leave:
        c.wait()
    wait_all(back, ret, send_b, recv_b, False)
    got = ret[...].astype(F32)
    for i in range(3):
        out_ref[i] = got[:, 8 * i : 8 * i + 8, :].reshape(devices * 8, width).astype(BF16)
    wait_all(back, ret, send_b, recv_b, True)


def final_kernel(local_ref, modes_ref, inv_ref, out_ref):
    part = jnp.dot(inv_ref[...], modes_ref[0], preferred_element_type=F32)
    out_ref[0] = jax.nn.gelu(local_ref[0].astype(F32) + part).astype(BF16)


def body(devices, fwd_np, inv_np, leg_np, state, filters, blocks, mix, gain, weight):
    cycles, lon, ch = state.shape
    lat_count = cycles * devices
    fwd, inv = jnp.asarray(fwd_np), jnp.asarray(inv_np)
    if leg_np is not None:
        ana, syn = jnp.asarray(leg_np[0]), jnp.asarray(leg_np[1])
    else:
        own = lax.axis_index("lat") * M_DEV + jnp.arange(M_DEV, dtype=jnp.int32)
        theta = (jnp.arange(lat_count, dtype=F32) + 0.5) * (math.pi / lat_count)
        quad = jnp.sin(theta) * (2.0 * math.pi * math.pi / lat_count)
        ana, syn = spread(jnp, legendre_table(own, lat_count, lat_count), quad, devices)
        ana, syn = ana.astype(BF16)[None], syn.astype(BF16)[None]

    vmem = pl.BlockSpec(memory_space=pltpu.VMEM)
    smem = pl.BlockSpec(memory_space=pltpu.SMEM)
    hbm = pl.BlockSpec(memory_space=pl.ANY)
    shape = jax.ShapeDtypeStruct
    block = pltpu.VMEM((devices, BLK, ch), BF16)
    thin = pltpu.VMEM((devices, 16, ch), BF16)
    cycle = pltpu.VMEM((lon // 8, 16, ch), BF16)
    rows = 2 * M_DEV * CHUNK
    sems = pltpu.SemaphoreType.DMA((devices,))
    turned = jnp.transpose(blocks, (0, 2, 1))
    local, modes = pl.pallas_call(
        functools.partial(main_kernel, devices),
        out_shape=(shape((cycles, lon, ch), BF16), shape((3, devices * 8, ch), BF16)),
        in_specs=[smem, smem, smem] + [hbm] * 7,
        out_specs=(hbm, vmem),
        scratch_shapes=[
            pltpu.VMEM((cycles, lon, ch), BF16),
            pltpu.VMEM(mix.shape, BF16),
            pltpu.VMEM(fwd.shape, BF16),
            pltpu.VMEM(gain.shape, F32),
            pltpu.VMEM(weight.shape, BF16),
            pltpu.SemaphoreType.DMA((4,)),
            pltpu.SemaphoreType.DMA((3,)),
            cycle, cycle, cycle, cycle, cycle,
            pltpu.VMEM((3, KB * ROWS, 6 * WIN), BF16),
            pltpu.VMEM((3, lon, KB * ch), BF16),
            pltpu.VMEM((2, lon // ROWS, KB * ROWS, ch), F32),
            thin, thin, thin, thin, block, block,
            pltpu.VMEM((rows, devices * BLK), BF16),
            pltpu.VMEM((devices * BLK, rows), BF16),
            pltpu.VMEM((2 * ch, 2 * ch), BF16),
            pltpu.VMEM((devices * BLK, ch), F32),
            pltpu.SemaphoreType.DMA((2,)),
            pltpu.SemaphoreType.DMA((6,)),
            pltpu.SemaphoreType.DMA((2,)),
            pltpu.SemaphoreType.DMA((2,)),
            sems, sems, sems, sems, sems, sems,
        ],
        compiler_params=pltpu.CompilerParams(
            vmem_limit_bytes=60 * 2**20, collective_id=0, has_side_effects=True
        ),
        name="main",
    )(
        jnp.transpose(filters, (0, 1, 4, 2, 3)), lon // 16 - 1 - turned // 2, 16 - 8 * (turned % 2),
        state.reshape(cycles, lon // 16, 16, ch), mix, fwd, ana, syn, gain, weight,
    )
    step = 720
    return pl.pallas_call(
        final_kernel,
        grid=(3, lon // step),
        out_shape=shape((cycles, lon, ch), BF16),
        in_specs=[
            pl.BlockSpec((1, step, ch), lambda i, n: (i, n, 0)),
            pl.BlockSpec((1, devices * 8, ch), lambda i, n: (i, 0, 0)),
            pl.BlockSpec((step, devices * 8), lambda i, n: (n, 0)),
        ],
        out_specs=pl.BlockSpec((1, step, ch), lambda i, n: (i, n, 0)),
        compiler_params=pltpu.CompilerParams(vmem_limit_bytes=60 * 2**20),
        name="final",
    )(local, modes, inv)


def solution(mesh):
    devices = mesh.shape["lat"]
    lon = 1440
    fwd, inv = constants(devices, lon)
    count = M_DEV * devices
    leg = None
    if count <= 96:
        table = legendre_np(count)
        quad = np.sin((np.arange(count) + 0.5) * (math.pi / count)) * (2.0 * math.pi**2 / count)
        pairs = [spread(np, table[M_DEV * d : M_DEV * d + M_DEV], quad, devices) for d in range(devices)]
        leg = [np.stack([p[n] for p in pairs]).astype(np.float32).astype(ml_dtypes.bfloat16) for n in range(2)]
    return jax.shard_map(
        functools.partial(body, devices, fwd, inv, leg),
        mesh=mesh,
        in_specs=(
            P(("groups", "lat"), None, None),
            P("lat", None, None, None, None),
            P("lat", None, None),
            P(),
            P(),
            P(),
        ),
        out_specs=P(("groups", "lat"), None, None),
        check_vma=False,
    )
```

```python
import functools
import math

import jax
import jax.numpy as jnp
import ml_dtypes
import numpy as np
from jax import lax
from jax.experimental import pallas as pl
from jax.experimental.pallas import tpu as pltpu
from jax.sharding import PartitionSpec as P

M_DEV = 3
KB = 3
SB = 8
ROWS = 48
WIN = 64
CHUNK = 48
BLK = 32
log_cut = -69.0
MESH = pl.DeviceIdType.MESH
F32 = jnp.float32
BF16 = jnp.bfloat16


def legendre_np(count):
    theta = (np.arange(count) + 0.5) * (math.pi / count)
    cosine, sine = np.cos(theta)[None], np.sin(theta)[None]
    m = np.arange(count, dtype=np.float64)[:, None]
    lg = np.array([math.lgamma(x + 0.5) - math.lgamma(x + 1.0) for x in range(count)])[:, None]
    g = 0.5 * (np.log(2 * m + 1) - math.log(4 * math.pi)) + 0.5 * (lg - 0.5 * math.log(math.pi)) + m * np.log(sine)
    first = np.where(g < log_cut, 0.0, np.exp(g))
    table = np.zeros((count, count, count))
    before = current = np.zeros((count, count))
    for l in range(count):
        up = np.sqrt((4.0 * l * l - 1.0) / np.maximum(l * l - m * m, 1.0)) if l else 0.0 * m
        down = np.sqrt(np.maximum((l - 1.0) ** 2 - m * m, 0.0) / max(4.0 * (l - 1.0) ** 2 - 1.0, 1.0))
        general = up * (cosine * current - down * before)
        second = np.sqrt(2 * m + 3) * cosine * current
        value = np.where(l < m, 0.0, np.where(l == m, first, np.where(l == m + 1, second, general)))
        before, current = current, value
        table[:, l] = value
    return table


def legendre_table(wave_orders, degree_count, lat_count):
    colatitude = (jnp.arange(lat_count, dtype=F32) + 0.5) * (math.pi / lat_count)
    cosine = jnp.cos(colatitude)[None, :]
    sine_col = jnp.sin(colatitude)[None, :]
    orders = wave_orders.astype(F32)[:, None]
    log_first = (
        0.5 * (jnp.log(2.0 * orders + 1.0) - math.log(4.0 * math.pi))
        + 0.5 * (lax.lgamma(orders + 0.5) - 0.5 * math.log(math.pi) - lax.lgamma(orders + 1.0))
        + orders * jnp.log(sine_col)
    )
    first_term = jnp.where(log_first < log_cut, 0.0, jnp.exp(log_first))

    def advance(state_pair, degree):
        before, current = state_pair
        deg_sq = degree * degree
        ord_sq = orders * orders
        lower_deg = degree - 1.0
        coef_up = jnp.sqrt(jnp.maximum(4.0 * deg_sq - 1.0, 0.0) / jnp.maximum(deg_sq - ord_sq, 1.0))
        coef_down = jnp.sqrt(
            jnp.maximum(lower_deg * lower_deg - ord_sq, 0.0)
            / jnp.maximum(4.0 * lower_deg * lower_deg - 1.0, 1.0)
        )
        general = coef_up * (cosine * current - coef_down * before)
        second = jnp.sqrt(2.0 * orders + 3.0) * cosine * current
        next_value = jnp.where(
            degree < orders,
            0.0,
            jnp.where(
                degree == orders, first_term, jnp.where(degree == orders + 1.0, second, general)
            ),
        )
        return ((current, next_value), next_value)

    zeros_state = jnp.zeros((orders.shape[0], lat_count), F32)
    degrees = jnp.arange(degree_count, dtype=F32)
    _, table_rows = lax.scan(advance, (zeros_state, zeros_state), degrees)
    return jnp.transpose(table_rows, (1, 0, 2))


def spread(xp, table, quad, devices):
    count = table.shape[1]
    chunks = count // CHUNK
    lat = xp.arange(count)[:, None]
    col = xp.arange(devices * BLK)[None, :]
    here = (lat == 3 * (col // BLK) + col % BLK // 8) & (col % BLK < 24)
    per = devices * 16
    late = col // per
    source = xp.where(late == 0, 1, 2 * (col % 16 // 8))
    there = (lat == 3 * (col % per // 16) + source) & ((late == 1) | (col % 16 < 8))

    def lay(values, here):
        if xp is jnp:
            values = values.astype(BF16)
        rows = []
        for p in range(2):
            for m in range(M_DEV):
                pick = (here & (col % 8 == 2 * m + p)).astype(values.dtype)
                rows.append(xp.matmul(values[m], pick).reshape(chunks, 1, CHUNK, devices * BLK))
        return xp.concatenate(rows, axis=1).reshape(chunks, 2 * M_DEV * CHUNK, devices * BLK)

    return lay(table * quad[None, None, :], there), lay(table, here).transpose(0, 2, 1)


def constants(devices, lon):
    modes = M_DEV * devices
    angle = (np.arange(modes)[:, None] * np.arange(lon)[None, :] % lon) * (2.0 * math.pi / lon)
    factor = np.where(np.arange(modes) == 0, 1.0, 2.0)[:, None]

    def pad(re, im):
        paired = np.stack([re, im], axis=1).reshape(devices, 2 * M_DEV, lon)
        return np.pad(paired, ((0, 0), (0, 2), (0, 0))).reshape(devices * 8, lon)

    bf = ml_dtypes.bfloat16
    fwd = pad(np.cos(angle) / lon, -np.sin(angle) / lon).astype(np.float32).astype(bf)
    inv = pad(factor * np.cos(angle), -factor * np.sin(angle)).T.astype(np.float32).astype(bf)
    return fwd, inv


def fill_toeplitz(t_ref, f_ref, o_ref, cycle, offset, column):
    shape = (ROWS, 2 * WIN)
    lane = lax.broadcasted_iota(jnp.int32, shape, 1)
    first_slot = lane < WIN
    off = [o_ref[cycle, slot, offset] for slot in range(2)]
    delta = (
        lax.broadcasted_iota(jnp.int32, shape, 0)
        + jnp.where(first_slot, off[0], off[1] + WIN)
        - lane
    )
    parts = [jnp.zeros(shape, F32) for _ in range(KB)]
    for t in range(SB):
        hit = delta == t
        for k in range(KB):
            value = jnp.where(first_slot, f_ref[cycle, offset, k, 0, t], f_ref[cycle, offset, k, 1, t])
            parts[k] = jnp.where(hit, value, parts[k])
    for k in range(KB):
        t_ref[cycle, k * ROWS : (k + 1) * ROWS, column * 2 * WIN : (column + 1) * 2 * WIN] = parts[k].astype(BF16)


def windows(b_ref, ref, cycle, offset, a):
    pieces = []
    for slot in range(2):
        row = b_ref[cycle, slot, offset] + a * (ROWS // 16)
        pieces += [ref[row + n] for n in range(WIN // 16)]
    return pieces


def main_kernel(
    devices, f_ref, b_ref, o_ref, x_hbm, mix_hbm, fwd_hbm, ana_hbm, syn_hbm, gain_hbm, w_hbm,
    loc_hbm, out_ref,
    loc_ref, mix_ref, fwd_ref, gain_ref, w_ref, own_sem, loc_sem,
    e0, e1, e2, north, south, tab, bas, part,
    x_mid, x_ref, recv_mid, recv, back, ret, ana, syn, wide, acc,
    load_sem, x_sem, halo_send, halo_recv, send_a, recv_a, send_b, recv_b, send_c, recv_c,
):
    me = lax.axis_index("lat")
    tiles = x_hbm.shape[1]
    lon = tiles * 16
    chunks = ana_hbm.shape[1]
    mine = me if ana_hbm.shape[0] > 1 else 0
    width = w_ref.shape[2]
    half = M_DEV * CHUNK

    barrier = pltpu.get_barrier_semaphore()

    def greet(s, carry):
        pl.semaphore_signal(barrier, inc=1, device_id={"lat": lax.rem(me + s, devices)}, device_id_type=MESH)
        return carry

    lax.fori_loop(1, devices, greet, 0)

    held = (e0, e1, e2)
    fetches = []
    for i in range(3):
        fetches.append(pltpu.make_async_copy(x_hbm.at[i], held[i].at[pl.ds(0, tiles)], x_sem.at[2 * i]))
        fetches.append(
            pltpu.make_async_copy(x_hbm.at[i], held[i].at[pl.ds(tiles, tiles)], x_sem.at[2 * i + 1])
        )
    for c in fetches:
        c.start()
    small = [
        pltpu.make_async_copy(src, dst, own_sem.at[n])
        for n, (src, dst) in enumerate(
            ((w_hbm, w_ref), (mix_hbm, mix_ref), (fwd_hbm, fwd_ref), (gain_hbm, gain_ref))
        )
    ]
    for c in small:
        c.start()

    def load(ch):
        return (
            pltpu.make_async_copy(ana_hbm.at[mine, ch], ana, load_sem.at[0]),
            pltpu.make_async_copy(syn_hbm.at[mine, ch], syn, load_sem.at[1]),
        )

    for c in load(0):
        c.start()
    pl.semaphore_wait(barrier, devices - 1)

    send_up = pltpu.make_async_remote_copy(
        src_ref=x_hbm.at[2], dst_ref=north.at[pl.ds(0, tiles)], send_sem=halo_send.at[0], recv_sem=halo_recv.at[0],
        device_id={"lat": lax.rem(me + 1, devices)}, device_id_type=MESH,
    )
    send_down = pltpu.make_async_remote_copy(
        src_ref=x_hbm.at[0], dst_ref=south.at[pl.ds(0, tiles)], send_sem=halo_send.at[1], recv_sem=halo_recv.at[1],
        device_id={"lat": lax.rem(me + devices - 1, devices)}, device_id_type=MESH,
    )

    @pl.when(me < devices - 1)
    def _():
        send_up.start()

    @pl.when(me > 0)
    def _():
        send_down.start()

    plan = {0: ((0, 1), (1, 2)), 1: ((0, 0), (1, 1), (2, 2)), 2: ((1, 0), (2, 1))}
    for i in range(3):
        for n, (_, offset) in enumerate(plan[i]):
            fill_toeplitz(tab, f_ref, o_ref, i, offset, n)
    fill_toeplitz(tab, f_ref, o_ref, 0, 0, 2)
    fill_toeplitz(tab, f_ref, o_ref, 2, 2, 2)
    for c in small:
        c.wait()
    wide[0:width, 0:width] = w_ref[0]
    wide[0:width, width:] = w_ref[1]
    wide[width:, 0:width] = -w_ref[1]
    wide[width:, width:] = w_ref[0]
    acc[...] = jnp.zeros_like(acc)
    for c in fetches:
        c.wait()

    def keep(i, first, basis):
        basis = basis.astype(BF16)
        for k in range(KB):
            bas[i, pl.ds(first, ROWS), k * width : (k + 1) * width] = basis[k * ROWS : (k + 1) * ROWS]

    def inner(a, carry):
        first = pl.multiple_of(a * ROWS, 16)
        for i in range(3):
            pieces = []
            for source, offset in plan[i]:
                pieces += windows(b_ref, held[source], i, offset, a)
            used = len(pieces) * 16
            basis = jnp.dot(tab[i, :, 0:used], jnp.concatenate(pieces, axis=0), preferred_element_type=F32)
            if i == 1:
                keep(i, first, basis)
            else:
                part[i // 2, a] = basis
        return carry

    lax.fori_loop(0, lon // ROWS, inner, 0)

    def remote(src, dst, ssem, rsem, s, to, row):
        return pltpu.make_async_remote_copy(
            src_ref=src.at[to], dst_ref=dst.at[row], send_sem=ssem.at[s], recv_sem=rsem.at[row],
            device_id={"lat": to}, device_id_type=MESH,
        )

    def start_all(src, dst, ssem, rsem):
        def one(s, carry):
            remote(src, dst, ssem, rsem, s, lax.rem(me + s, devices), me).start()
            return carry

        lax.fori_loop(1, devices, one, 0)
        dst[me] = src[me]

    def wait_all(src, dst, ssem, rsem, send):
        def one(s, carry):
            peer = lax.rem(me + s, devices)
            copy = remote(src, dst, ssem, rsem, s, peer, peer)
            if send:
                copy.wait_send()
            else:
                copy.wait_recv()
            return carry

        lax.fori_loop(1, devices, one, 0)

    step = lon // 3

    leave = [pltpu.make_async_copy(loc_ref.at[i], loc_hbm.at[i], loc_sem.at[i]) for i in range(3)]

    def mix_cycle(i):
        def one(n, carry):
            at = pl.ds(pl.multiple_of(n * step, 16), step)
            loc_ref[i, at, :] = jnp.dot(bas[i, at, :], mix_ref[...], preferred_element_type=F32).astype(BF16)
            return carry

        lax.fori_loop(0, 3, one, 0)
        leave[i].start()
        return jnp.dot(fwd_ref[...], loc_ref[i], preferred_element_type=F32)

    mid = mix_cycle(1).reshape(devices, 8, width)
    x_mid[...] = jnp.concatenate([mid, jnp.zeros_like(mid)], axis=1).astype(BF16)
    start_all(x_mid, recv_mid, send_c, recv_c)

    for ref, inside, copy in ((north, me > 0, send_up), (south, me < devices - 1, send_down)):
        @pl.when(inside)
        def _(copy=copy):
            copy.wait_recv()

        @pl.when(jnp.logical_not(inside))
        def _(ref=ref):
            ref[0:tiles] = jnp.zeros((tiles, 16, width), BF16)

        ref[tiles : 2 * tiles] = ref[0:tiles]

    def outer(group, carry):
        work = []
        for a in (3 * group, 3 * group + 1, 3 * group + 2):
            for h, ref in enumerate((north, south)):
                data = jnp.concatenate(windows(b_ref, ref, 2 * h, 2 * h, a), axis=0)
                basis = jnp.dot(tab[2 * h, :, 4 * WIN :], data, preferred_element_type=F32)
                work.append((h, a, basis + part[h, a]))
        for h, a, basis in work:
            keep(2 * h, pl.multiple_of(a * ROWS, 16), basis)
        return carry

    lax.fori_loop(0, lon // ROWS // 3, outer, 0)
    s0 = mix_cycle(0)
    s2 = mix_cycle(2)
    pair = [s.reshape(devices, 8, width) for s in (s0, s2)]
    x_ref[...] = jnp.concatenate(pair, axis=1).astype(BF16)
    start_all(x_ref, recv, send_a, recv_a)

    @pl.when(me < devices - 1)
    def _():
        send_up.wait_send()

    @pl.when(me > 0)
    def _():
        send_down.wait_send()

    wait_all(x_mid, recv_mid, send_c, recv_c, False)
    wait_all(x_ref, recv, send_a, recv_a, False)

    rows = 16 * BLK

    def chunk(ch, carry):
        for c in load(ch):
            c.wait()
        data = jnp.concatenate(
            [ref[...].reshape(devices * 16, width) for ref in (recv_mid, recv)], axis=0
        )
        coef = jnp.dot(ana[...], data, preferred_element_type=F32)
        gain = gain_ref[pl.ds(pl.multiple_of(ch * CHUNK, CHUNK), CHUNK), :]
        gain = jnp.concatenate([gain] * M_DEV, axis=0)
        scaled = jnp.concatenate([coef[:half] * gain, coef[half:] * gain], axis=1).astype(BF16)
        mixed = jnp.dot(scaled, wide[...], preferred_element_type=F32).astype(BF16)
        stacked = jnp.concatenate([mixed[:, :width], mixed[:, width:]], axis=0)

        def piece(r, inner_carry):
            at = pl.ds(pl.multiple_of(r * rows, rows), rows)
            acc[at, :] += jnp.dot(syn[at, :], stacked, preferred_element_type=F32)
            return inner_carry

        lax.fori_loop(0, devices * BLK // rows, piece, 0)

        @pl.when(ch + 1 < chunks)
        def _():
            for c in load(ch + 1):
                c.start()

        return carry

    lax.fori_loop(0, chunks, chunk, 0)
    back[...] = acc[...].reshape(devices, BLK, width).astype(BF16)
    start_all(back, ret, send_b, recv_b)
    wait_all(x_mid, recv_mid, send_c, recv_c, True)
    wait_all(x_ref, recv, send_a, recv_a, True)
    for c in leave:
        c.wait()
    wait_all(back, ret, send_b, recv_b, False)
    got = ret[...].astype(F32)
    for i in range(3):
        out_ref[i] = got[:, 8 * i : 8 * i + 8, :].reshape(devices * 8, width).astype(BF16)
    wait_all(back, ret, send_b, recv_b, True)


def final_kernel(local_ref, modes_ref, inv_ref, out_ref):
    part = jnp.dot(inv_ref[...], modes_ref[0], preferred_element_type=F32)
    out_ref[0] = jax.nn.gelu(local_ref[0].astype(F32) + part).astype(BF16)


def body(devices, fwd_np, inv_np, leg_np, state, filters, blocks, mix, gain, weight):
    cycles, lon, ch = state.shape
    lat_count = cycles * devices
    fwd, inv = jnp.asarray(fwd_np), jnp.asarray(inv_np)
    if leg_np is not None:
        ana, syn = jnp.asarray(leg_np[0]), jnp.asarray(leg_np[1])
    else:
        own = lax.axis_index("lat") * M_DEV + jnp.arange(M_DEV, dtype=jnp.int32)
        theta = (jnp.arange(lat_count, dtype=F32) + 0.5) * (math.pi / lat_count)
        quad = jnp.sin(theta) * (2.0 * math.pi * math.pi / lat_count)
        ana, syn = spread(jnp, legendre_table(own, lat_count, lat_count), quad, devices)
        ana, syn = ana.astype(BF16)[None], syn.astype(BF16)[None]

    vmem = pl.BlockSpec(memory_space=pltpu.VMEM)
    smem = pl.BlockSpec(memory_space=pltpu.SMEM)
    hbm = pl.BlockSpec(memory_space=pl.ANY)
    shape = jax.ShapeDtypeStruct
    block = pltpu.VMEM((devices, BLK, ch), BF16)
    thin = pltpu.VMEM((devices, 16, ch), BF16)
    cycle = pltpu.VMEM((lon // 8, 16, ch), BF16)
    rows = 2 * M_DEV * CHUNK
    sems = pltpu.SemaphoreType.DMA((devices,))
    turned = jnp.transpose(blocks, (0, 2, 1))
    local, modes = pl.pallas_call(
        functools.partial(main_kernel, devices),
        out_shape=(shape((cycles, lon, ch), BF16), shape((3, devices * 8, ch), BF16)),
        in_specs=[smem, smem, smem] + [hbm] * 7,
        out_specs=(hbm, vmem),
        scratch_shapes=[
            pltpu.VMEM((cycles, lon, ch), BF16),
            pltpu.VMEM(mix.shape, BF16),
            pltpu.VMEM(fwd.shape, BF16),
            pltpu.VMEM(gain.shape, F32),
            pltpu.VMEM(weight.shape, BF16),
            pltpu.SemaphoreType.DMA((4,)),
            pltpu.SemaphoreType.DMA((3,)),
            cycle, cycle, cycle, cycle, cycle,
            pltpu.VMEM((3, KB * ROWS, 6 * WIN), BF16),
            pltpu.VMEM((3, lon, KB * ch), BF16),
            pltpu.VMEM((2, lon // ROWS, KB * ROWS, ch), F32),
            thin, thin, thin, thin, block, block,
            pltpu.VMEM((rows, devices * BLK), BF16),
            pltpu.VMEM((devices * BLK, rows), BF16),
            pltpu.VMEM((2 * ch, 2 * ch), BF16),
            pltpu.VMEM((devices * BLK, ch), F32),
            pltpu.SemaphoreType.DMA((2,)),
            pltpu.SemaphoreType.DMA((6,)),
            pltpu.SemaphoreType.DMA((2,)),
            pltpu.SemaphoreType.DMA((2,)),
            sems, sems, sems, sems, sems, sems,
        ],
        compiler_params=pltpu.CompilerParams(
            vmem_limit_bytes=60 * 2**20, collective_id=0, has_side_effects=True
        ),
        name="main",
    )(
        jnp.transpose(filters, (0, 1, 4, 2, 3)), lon // 16 - 1 - turned // 2, 16 - 8 * (turned % 2),
        state.reshape(cycles, lon // 16, 16, ch), mix, fwd, ana, syn, gain, weight,
    )
    step = 480
    return pl.pallas_call(
        final_kernel,
        grid=(3, lon // step),
        out_shape=shape((cycles, lon, ch), BF16),
        in_specs=[
            pl.BlockSpec((1, step, ch), lambda i, n: (i, n, 0)),
            pl.BlockSpec((1, devices * 8, ch), lambda i, n: (i, 0, 0)),
            pl.BlockSpec((step, devices * 8), lambda i, n: (n, 0)),
        ],
        out_specs=pl.BlockSpec((1, step, ch), lambda i, n: (i, n, 0)),
        compiler_params=pltpu.CompilerParams(vmem_limit_bytes=60 * 2**20),
        name="final",
    )(local, modes, inv)


def solution(mesh):
    devices = mesh.shape["lat"]
    lon = 1440
    fwd, inv = constants(devices, lon)
    count = M_DEV * devices
    leg = None
    if count <= 96:
        table = legendre_np(count)
        quad = np.sin((np.arange(count) + 0.5) * (math.pi / count)) * (2.0 * math.pi**2 / count)
        pairs = [spread(np, table[M_DEV * d : M_DEV * d + M_DEV], quad, devices) for d in range(devices)]
        leg = [np.stack([p[n] for p in pairs]).astype(np.float32).astype(ml_dtypes.bfloat16) for n in range(2)]
    return jax.shard_map(
        functools.partial(body, devices, fwd, inv, leg),
        mesh=mesh,
        in_specs=(
            P(("groups", "lat"), None, None),
            P("lat", None, None, None, None),
            P("lat", None, None),
            P(),
            P(),
            P(),
        ),
        out_specs=P(("groups", "lat"), None, None),
        check_vma=False,
    )
```
